32 devices in a mesh: node: 16 (over z, y, x), local: 2 (over core).
Axes of the slice: x: 2, y: 2, z: 4, core: 2. Of those that a mesh axis runs over, the one named last changes fastest.
Arguments:
- tokens: bfloat16 [4096, 8192], P(('node', 'local')), may hold values from -6 to 6
- norm_gain: bfloat16 [8192], replicated, may hold values from 0.099609375 to 1.8984375
- key_weight: bfloat16 [8192, 128], P(('node', 'local')), may hold values from -0.0625 to 0.0625
- key_cotangent: bfloat16 [4096, 128], P(('node', 'local')), may hold values from -6 to 6
Outputs:
- keys: bfloat16 [4096, 128], P(('node', 'local'))
- token_grad: bfloat16 [4096, 8192], P(('node', 'local'))
- weight_grad: float32 [8192, 128], P(('node', 'local'))
- gain_grad: float32 [8192], replicated
The draws below stay inside these ranges and needn't reach their ends.
All inputs are finite; a program needn't handle non-finite values.
Results may differ from the reference program's by a relative error of at most 0.005.
Values may be sent and summed in bfloat16 or wider, within the bound.
A program may use at most 64 MiB of HBM per device.

```python
import math
import jax
import jax.numpy as jnp
from jax import lax

D = 8192
HD = 128
TOKENS = 4096


def strengthened(values, key, source, target, shards_of, factor):
    def block_of(axis_at):
        return (jnp.arange(values.shape[axis_at]) // (values.shape[axis_at] // shards_of)).reshape((-1,) + (1,) * (values.ndim - 1 - axis_at))

    first = jax.random.permutation(key, shards_of)[block_of(target)]
    far = (block_of(target) + shards_of // 2) % shards_of
    return jnp.where((block_of(source) == first) | (block_of(source) == far), factor * values, values)


def steps_of(rng, shape, shards, smallest, largest):
    gain = 1.0
    for dim, parts in shards:
        heights = jax.random.uniform(jax.random.fold_in(jax.random.fold_in(rng, 6), dim), (parts,), jnp.float32, smallest / len(shards), largest / len(shards))
        gain = gain * jnp.repeat(jnp.exp(heights), shape[dim] // parts).reshape((-1,) + (1,) * (len(shape) - 1 - dim))
    return gain


def noise(rng, shape, deviation, limit, split=(), kind=jnp.bfloat16):
    level = steps_of(rng, shape, split, -0.22, 0.18) if split else 1.0
    array = jax.random.normal(rng, shape, jnp.float32) * deviation * level
    return jnp.minimum(jnp.maximum(array, -limit), limit).astype(kind)


def gaussian_with(key, extent, spread, most, pieces, heavy, held_as=jnp.bfloat16):
    drawn = spread * jax.random.normal(key, extent, jnp.float32)
    if pieces:
        drawn = drawn * steps_of(key, extent, pieces, -0.22, 0.18)
    return jnp.clip(strengthened(drawn, jax.random.fold_in(key, 3), *heavy), -most, most).astype(held_as)


def setup_inputs(seed: int = 0) -> dict:
    key_of = jax.random.split(jax.random.key(seed), 5)
    return {
        "tokens": gaussian_with(key_of[0], (TOKENS, D), 1.0, 6.0, ((0, 32),), (0, 1, 32, 2.75)),
        "norm_gain": jnp.clip(1.0 + 0.18 * jax.random.normal(key_of[1], (D,), jnp.float32), 0.099609375, 1.8984375).astype(jnp.bfloat16),
        "key_weight": noise(key_of[2], (D, HD), D ** -0.5, 0.0625, ((0, 32),)),
        "key_cotangent": noise(key_of[3], (TOKENS, HD), 1.0, 6.0, ((0, 32),)),
    }


def reference(tokens, norm_gain, key_weight, key_cotangent):
    block = math.gcd(TOKENS, 4096)
    count = TOKENS // block
    gain_wide = norm_gain.astype(jnp.float32)
    scale = 1.0 / math.sqrt(TOKENS)

    def step(carry, items):
        weight_sum, gain_sum = carry
        rows, cot_rows = items
        wide = rows.astype(jnp.float32)
        rstd = lax.rsqrt(lax.optimization_barrier(jnp.mean(wide * wide, axis=1, keepdims=True)) + 1e-05)
        normed = wide * rstd
        hidden = (normed * gain_wide).astype(jnp.bfloat16)
        keys = jnp.dot(hidden, key_weight, preferred_element_type=jnp.float32).astype(jnp.bfloat16)
        dhidden = lax.dot_general(cot_rows, key_weight, (((1,), (1,)), ((), ())), preferred_element_type=jnp.float32)
        dnormed = dhidden * gain_wide
        inner = lax.optimization_barrier(jnp.mean(dnormed * normed, axis=1, keepdims=True))
        token_grad = (rstd * (dnormed - normed * inner)).astype(jnp.bfloat16)
        weight_sum = weight_sum + lax.dot_general(hidden, cot_rows, (((0,), (0,)), ((), ())), preferred_element_type=jnp.float32)
        gain_sum = gain_sum + lax.optimization_barrier(jnp.sum(dhidden * normed, axis=0))
        return ((weight_sum, gain_sum), (keys, token_grad))
    start = (jnp.zeros((D, HD), jnp.float32), jnp.zeros((D,), jnp.float32))
    (weight_sum, gain_sum), (keys, token_grad) = lax.scan(step, start, (tokens.reshape(count, block, D), key_cotangent.reshape(count, block, HD)))
    return (keys.reshape(TOKENS, HD), token_grad.reshape(TOKENS, D), weight_sum * scale, gain_sum * scale)
```

```python
import functools
import math

import jax
import jax.numpy as jnp
from jax import lax
from jax.experimental import pallas as pl
from jax.experimental.pallas import tpu as pltpu
from jax.sharding import PartitionSpec as P

MESH = pl.DeviceIdType.MESH
F32 = jnp.float32
BF16 = jnp.bfloat16


def stream_plan(bits, rows):
    rest = list(range(1, bits))
    if bits == 5 and rows % 256 == 0:
        unit = rows // 8
        sizes = [3 * unit, 3 * unit, 2 * unit]
        orders = [[0, 1, 2, 3, 4], [0, 2, 3, 4, 1], [0, 3, 4, 1, 2]]
    else:
        sizes = [rows // 2, rows // 2]
        orders = [[0] + rest, [0] + rest[::-1]]
    return sizes, orders


def kernel(
    plan, local_count, scale, tok_hbm, gain_ref, w_ref, cot_ref,
    keys_ref, tg_hbm, wg_ref, gg_ref,
    tok, hid, tg, gains, rstds, rowco, gmine, gall, *rest,
):
    sizes, orders = plan
    bits = len(orders[0])
    count = 1 << bits
    streams = len(sizes)
    offs = [sum(sizes[:s]) for s in range(streams)]
    rows, heads = w_ref.shape
    toks, width = tok.shape
    it = iter(rest)
    wbuf = [next(it) for _ in range(streams)]
    acc = [next(it) for _ in range(streams)]
    send = [[next(it) for _ in range(bits)] for _ in range(streams)]
    recv = [[next(it) for _ in range(bits)] for _ in range(streams)]
    (tok_sem, tg_sem, ag_send, ag_recv, rs_send, rs_recv, g_send, g_recv) = list(it)

    me = lax.axis_index("node") * local_count + lax.axis_index("local")
    mine = [(me // (1 << k)) % 2 for k in range(bits)]

    def device(index):
        return (index // local_count, index % local_count)

    def partner(bit):
        return device(me + (1 << bit) * (1 - 2 * mine[bit]))

    def block_of(r):
        total = 0
        for k in range(bits):
            total = total + (1 << k) * ((mine[k] + r // (1 << k)) % 2)
        return total

    def place(s, r):
        total = 0
        for j, k in enumerate(orders[s]):
            total = total + (1 << (bits - 1 - j)) * ((r // (1 << k)) % 2)
        return total

    def columns(i):
        return pl.ds(pl.multiple_of(i * rows, rows), rows)

    def gain_of(i):
        parts = rows // 128
        return jnp.concatenate(
            [gains[pl.ds(i * parts + j, 1), :] for j in range(parts)], axis=1
        )

    chunks = tok_sem.shape[0]
    cw = width // chunks
    tok_copies = [
        pltpu.make_async_copy(
            tok_hbm.at[:, pl.ds(c * cw, cw)], tok.at[:, pl.ds(c * cw, cw)], tok_sem.at[c]
        )
        for c in range(chunks)
    ]
    for copy in tok_copies:
        copy.start()

    barrier = pltpu.get_barrier_semaphore()

    def greet(j, carry):
        pl.semaphore_signal(
            barrier, inc=1, device_id=device((me + j) % count), device_id_type=MESH
        )
        return carry

    lax.fori_loop(1, count, greet, 0)
    for s in range(streams):
        wbuf[s][0] = w_ref[pl.ds(offs[s], sizes[s]), :]
    gains[...] = gain_ref[...].astype(F32)
    pl.semaphore_wait(barrier, count - 1)

    def ag_copy(s, k):
        size = 1 << k
        return pltpu.make_async_remote_copy(
            src_ref=wbuf[s].at[pl.ds(0, size)],
            dst_ref=wbuf[s].at[pl.ds(size, size)],
            send_sem=ag_send.at[s, k],
            recv_sem=ag_recv.at[s, k],
            device_id=partner(orders[s][bits - 1 - k]),
            device_id_type=MESH,
        )

    def ag_step(k):
        for s in range(streams):
            if k:
                ag_copy(s, k - 1).wait_recv()
            if k < bits:
                ag_copy(s, k).start()

    def rs_copy(s, k):
        return pltpu.make_async_remote_copy(
            src_ref=send[s][k],
            dst_ref=recv[s][k],
            send_sem=rs_send.at[s, k],
            recv_sem=rs_recv.at[s, k],
            device_id=partner(orders[s][k]),
            device_id_type=MESH,
        )

    def rs_step(k):
        half = count >> (k + 1)
        for s in range(streams):
            rs_copy(s, k).wait_recv()
            low = half // 2
            if low:
                for p in range(low):
                    send[s][k + 1][p] = (
                        acc[s][low + p] + recv[s][k][low + p].astype(F32)
                    ).astype(BF16)
                rs_copy(s, k + 1).start()
                for p in range(low):
                    acc[s][p] = acc[s][p] + recv[s][k][p].astype(F32)

    ag_step(0)

    squares = jnp.zeros((toks, 128), F32)
    for c in range(chunks):
        tok_copies[c].wait()

        def square(j, total, c=c):
            part = tok[:, pl.ds(pl.multiple_of(c * cw + j * 256, 256), 256)].astype(F32)
            part = part * part
            return total + part[:, :128] + part[:, 128:]

        squares = lax.fori_loop(0, cw // 256, square, squares, unroll=2)
    rstd = lax.rsqrt(jnp.sum(squares, axis=1, keepdims=True) * (1.0 / width) + 1e-05)
    rstds[...] = jnp.broadcast_to(rstd, rstds.shape)

    ag_step(1)

    def weight_terms(flip):
        def body(q, carry):
            r = 2 * q + flip
            i = block_of(r)
            normed = tok[:, columns(i)].astype(F32) * rstds[:, :1]
            hidden = (normed * gain_of(i)).astype(BF16)
            hid[:, columns(i)] = hidden
            terms = lax.dot_general(
                hidden, cot_ref[...], (((0,), (0,)), ((), ())), preferred_element_type=F32
            )
            for s in range(streams):
                part = terms[offs[s]: offs[s] + sizes[s]]
                if flip:
                    send[s][0][place(s, r) - count // 2] = part.astype(BF16)
                else:
                    acc[s][place(s, r)] = part
            return carry

        lax.fori_loop(0, count // 2, body, 0, unroll=2)

    weight_terms(1)
    for s in range(streams):
        rs_copy(s, 0).start()
    ag_step(2)
    weight_terms(0)
    rs_step(0)
    for k in range(3, bits):
        ag_step(k)

    def weights(r):
        return jnp.concatenate([wbuf[s][place(s, r)] for s in range(streams)], axis=0)

    def keys_of(flip, total):
        def body(q, total):
            r = 2 * q + flip
            return total + jnp.dot(
                hid[:, columns(block_of(r))], weights(r), preferred_element_type=F32
            )

        return lax.fori_loop(0, count // 2, body, total, unroll=2)

    total = keys_of(0, jnp.zeros((toks, heads), F32))
    rs_step(1)
    ag_step(bits)
    total = keys_of(1, total)
    keys_ref[...] = total.astype(BF16)
    inner = jnp.sum(total * cot_ref[...].astype(F32), axis=1, keepdims=True) * (1.0 / width)
    back = rstds[:, :1]
    rowco[...] = jnp.broadcast_to(back * back * inner, rowco.shape)
    rs_step(2)

    groups = tg_sem.shape[0]
    gw = width // groups
    per = count // groups

    def tg_copy(g):
        return pltpu.make_async_copy(
            tg.at[:, pl.ds(g * gw, gw)], tg_hbm.at[:, pl.ds(g * gw, gw)], tg_sem.at[g]
        )

    def token_group(g):
        def body(q, carry):
            i = g * per + q
            r = block_of(i)
            dhidden = lax.dot_general(
                cot_ref[...], weights(r), (((1,), (1,)), ((), ())), preferred_element_type=F32
            )
            wide = tok[:, columns(i)].astype(F32)
            tg[:, columns(i)] = (
                dhidden * gain_of(i) * rstds[:, :1] - wide * rowco[:, :1]
            ).astype(BF16)
            return carry

        lax.fori_loop(0, per, body, 0, unroll=2)
        tg_copy(g).start()

    def gain_copy(j):
        return pltpu.make_async_remote_copy(
            src_ref=gmine,
            dst_ref=gall.at[me],
            send_sem=g_send.at[j],
            recv_sem=g_recv.at[j],
            device_id=device((me + j) % count),
            device_id_type=MESH,
        )

    def finish_weight():
        parts = []
        for s in range(streams):
            rs_copy(s, bits - 1).wait_recv()
            parts.append((acc[s][0] + recv[s][bits - 1][0].astype(F32)) * scale)
        grad = jnp.concatenate(parts, axis=0)
        wg_ref[...] = grad
        product = grad * w_ref[...].astype(F32)
        ones = jnp.ones((8, heads), F32)
        sums = lax.dot_general(
            ones, product, (((1,), (1,)), ((), ())),
            precision=lax.Precision.HIGHEST, preferred_element_type=F32,
        )
        own = sums[:1] / gain_of(me)
        gmine[...] = own
        gall[me] = own

        def give(j, carry):
            gain_copy(j).start()
            return carry

        lax.fori_loop(1, count, give, 0)

    steps = [functools.partial(rs_step, k) for k in range(3, bits - 1)] + [finish_weight]
    for g in range(groups):
        token_group(g)
        if g % 2 == 0 and steps:
            steps.pop(0)()
    for step in steps:
        step()

    def taken(j, carry):
        gain_copy(j).wait_recv()
        gain_copy(j).wait_send()
        return carry

    lax.fori_loop(1, count, taken, 0)
    parts = rows // 128
    for b in range(count):
        for j in range(parts):
            gg_ref[b * parts + j: b * parts + j + 1, :] = gall[b, :, j * 128: (j + 1) * 128]
    for s in range(streams):
        for k in range(bits):
            ag_copy(s, k).wait_send()
            rs_copy(s, k).wait_send()
    for g in range(groups):
        tg_copy(g).wait()


def fused(local_count, count, scale, tokens, norm_gain, key_weight, key_cotangent):
    rows, heads = key_weight.shape
    toks, width = tokens.shape
    bits = count.bit_length() - 1
    plan = stream_plan(bits, rows)
    sizes, _ = plan
    vmem = pl.BlockSpec(memory_space=pltpu.VMEM)
    hbm = pl.BlockSpec(memory_space=pl.ANY)
    stages = [
        pltpu.VMEM((count >> (k + 1), size, heads), BF16) for size in sizes for k in range(bits)
    ]
    keys, tg, wg, gg = pl.pallas_call(
        functools.partial(kernel, plan, local_count, scale),
        out_shape=(
            jax.ShapeDtypeStruct((toks, heads), BF16),
            jax.ShapeDtypeStruct((toks, width), BF16),
            jax.ShapeDtypeStruct((rows, heads), F32),
            jax.ShapeDtypeStruct((width // 128, 128), F32),
        ),
        in_specs=[hbm, vmem, vmem, vmem],
        out_specs=(vmem, hbm, vmem, vmem),
        scratch_shapes=[
            pltpu.VMEM((toks, width), BF16),
            pltpu.VMEM((toks, width), BF16),
            pltpu.VMEM((toks, width), BF16),
            pltpu.VMEM((width // 128, 128), F32),
            pltpu.VMEM((toks, 128), F32),
            pltpu.VMEM((toks, 128), F32),
            pltpu.VMEM((1, rows), F32),
            pltpu.VMEM((count, 1, rows), F32),
        ]
        + [pltpu.VMEM((count, size, heads), BF16) for size in sizes]
        + [pltpu.VMEM((count // 2, size, heads), F32) for size in sizes]
        + stages
        + stages
        + [
            pltpu.SemaphoreType.DMA((4,)),
            pltpu.SemaphoreType.DMA((8,)),
            pltpu.SemaphoreType.DMA((len(sizes), bits)),
            pltpu.SemaphoreType.DMA((len(sizes), bits)),
            pltpu.SemaphoreType.DMA((len(sizes), bits)),
            pltpu.SemaphoreType.DMA((len(sizes), bits)),
            pltpu.SemaphoreType.DMA((count,)),
            pltpu.SemaphoreType.DMA((count,)),
        ],
        compiler_params=pltpu.CompilerParams(
            collective_id=0, has_side_effects=True, vmem_limit_bytes=48 * 2**20
        ),
        cost_estimate=pl.CostEstimate(
            flops=6 * toks * width * heads, bytes_accessed=4 * toks * width, transcendentals=0
        ),
    )(tokens, norm_gain.reshape(width // 128, 128), key_weight, key_cotangent)
    return keys, tg, wg, gg.reshape(width)


def plain(scale, tokens, norm_gain, key_weight, key_cotangent):
    gain_wide = norm_gain.astype(F32)
    wide = tokens.astype(F32)
    rstd = lax.rsqrt(jnp.mean(wide * wide, axis=1, keepdims=True) + 1e-05)
    normed = wide * rstd
    hidden = (normed * gain_wide).astype(BF16)
    whole = lax.all_gather(key_weight, ("node", "local"), axis=0, tiled=True)
    keys = jnp.dot(hidden, whole, preferred_element_type=F32).astype(BF16)
    dhidden = lax.dot_general(
        key_cotangent, whole, (((1,), (1,)), ((), ())), preferred_element_type=F32
    )
    dnormed = dhidden * gain_wide
    inner = jnp.mean(dnormed * normed, axis=1, keepdims=True)
    token_grad = (rstd * (dnormed - normed * inner)).astype(BF16)
    gain_grad = lax.psum(jnp.sum(dhidden * normed, axis=0) * scale, ("node", "local"))
    terms = lax.dot_general(
        hidden, key_cotangent, (((0,), (0,)), ((), ())), preferred_element_type=F32
    )
    weight_grad = lax.psum_scatter(
        terms * scale, ("node", "local"), scatter_dimension=0, tiled=True
    )
    return keys, token_grad, weight_grad, gain_grad


def solution(mesh):
    local_count = mesh.shape["local"]
    count = mesh.shape["node"] * local_count

    def local(tokens, norm_gain, key_weight, key_cotangent):
        scale = 1.0 / math.sqrt(tokens.shape[0] * count)
        if key_weight.shape[0] % 128 == 0 and count & (count - 1) == 0 and count >= 16:
            return fused(
                local_count, count, scale, tokens, norm_gain, key_weight, key_cotangent
            )
        return plain(scale, tokens, norm_gain, key_weight, key_cotangent)

    placed = P(("node", "local"), None)
    return jax.shard_map(
        local,
        mesh=mesh,
        in_specs=(placed, P(), placed, placed),
        out_specs=(placed, placed, placed, P()),
        check_vma=False,
    )
```

```python
import functools
import math

import jax
import jax.numpy as jnp
from jax import lax
from jax.experimental import pallas as pl
from jax.experimental.pallas import tpu as pltpu
from jax.sharding import PartitionSpec as P

MESH = pl.DeviceIdType.MESH
F32 = jnp.float32
BF16 = jnp.bfloat16


def stream_plan(bits):
    rest = list(range(1, bits))
    if bits == 5:
        return [3, 3, 2], [[0, 1, 2, 3, 4], [0, 2, 3, 4, 1], [0, 3, 4, 1, 2]]
    return [4, 4], [[0] + rest, [0] + rest[::-1]]


def kernel(
    plan, local_count, scale, tok_hbm, gain_hbm, w_hbm, cot_hbm,
    keys_hbm, tg_hbm, wg_hbm, gg_hbm,
    keys_ref, tg_ref, wg_ref, gg_ref, tok, gain_ref, w_ref, cot_ref, hid, back, gains, rstds, rowco, gmine, gall, *rest,
):
    shares, orders = plan
    bits = len(orders[0])
    count = 1 << bits
    streams = len(shares)
    rows, heads = w_ref.shape
    toks, width = tok.shape
    wsize = [n * rows // 8 for n in shares]
    woff = [sum(wsize[:s]) for s in range(streams)]
    gsize = [n * heads // 8 for n in shares]
    goff = [sum(gsize[:s]) for s in range(streams)]
    it = iter(rest)
    wbuf = [next(it) for _ in range(streams)]
    acc = [next(it) for _ in range(streams)]
    send = [[next(it) for _ in range(bits)] for _ in range(streams)]
    recv = [[next(it) for _ in range(bits)] for _ in range(streams)]
    (tok_sem, in_sem, out_sem, ag_send, ag_recv, rs_send, rs_recv, g_send, g_recv) = list(it)

    me = lax.axis_index("node") * local_count + lax.axis_index("local")
    mine = [(me // (1 << k)) % 2 for k in range(bits)]

    def device(index):
        return (index // local_count, index % local_count)

    def partner(bit):
        return device(me + (1 << bit) * (1 - 2 * mine[bit]))

    def block_of(r):
        total = 0
        for k in range(bits):
            total = total + (1 << k) * ((mine[k] + r // (1 << k)) % 2)
        return total

    def place(s, r):
        total = 0
        for j, k in enumerate(orders[s]):
            total = total + (1 << (bits - 1 - j)) * ((r // (1 << k)) % 2)
        return total

    def columns(i):
        return pl.ds(pl.multiple_of(i * rows, rows), rows)

    parts = rows // 128

    def gain_of(i):
        return jnp.concatenate(
            [gains[pl.ds(i * parts + j, 1), :] for j in range(parts)], axis=1
        )

    def across(ref):
        return jnp.concatenate([ref[...]] * parts, axis=1)

    w_copy = pltpu.make_async_copy(w_hbm, w_ref, in_sem.at[0])
    cot_copy = pltpu.make_async_copy(cot_hbm, cot_ref, in_sem.at[1])
    gain_copy_in = pltpu.make_async_copy(gain_hbm, gain_ref, in_sem.at[2])
    chunks = tok_sem.shape[0]
    cw = width // chunks
    tok_copies = [
        pltpu.make_async_copy(
            tok_hbm.at[:, pl.ds(c * cw, cw)], tok.at[:, pl.ds(c * cw, cw)], tok_sem.at[c]
        )
        for c in range(chunks)
    ]
    for copy in [w_copy] + tok_copies + [cot_copy, gain_copy_in]:
        copy.start()

    barrier = pltpu.get_barrier_semaphore()

    def greet(j, carry):
        pl.semaphore_signal(
            barrier, inc=1, device_id=device((me + j) % count), device_id_type=MESH
        )
        return carry

    lax.fori_loop(1, count, greet, 0)
    w_copy.wait()
    for s in range(streams):
        wbuf[s][0] = w_ref[pl.ds(woff[s], wsize[s]), :]
    pl.semaphore_wait(barrier, count - 1)

    def ag_copy(s, k):
        size = 1 << k
        return pltpu.make_async_remote_copy(
            src_ref=wbuf[s].at[pl.ds(0, size)],
            dst_ref=wbuf[s].at[pl.ds(size, size)],
            send_sem=ag_send.at[s, k],
            recv_sem=ag_recv.at[s, k],
            device_id=partner(orders[s][bits - 1 - k]),
            device_id_type=MESH,
        )

    def ag_step(k):
        for s in range(streams):
            if k:
                ag_copy(s, k - 1).wait_recv()
            if k < bits:
                ag_copy(s, k).start()

    def rs_copy(s, k):
        return pltpu.make_async_remote_copy(
            src_ref=send[s][k],
            dst_ref=recv[s][k],
            send_sem=rs_send.at[s, k],
            recv_sem=rs_recv.at[s, k],
            device_id=partner(orders[s][k]),
            device_id_type=MESH,
        )

    def rs_step(k):
        half = count >> (k + 1)
        low = half // 2
        for s in range(streams):
            rs_copy(s, k).wait_recv()
            for p in range(low):
                send[s][k + 1][p] = (
                    acc[s][low + p] + recv[s][k][low + p].astype(F32)
                ).astype(BF16)
            rs_copy(s, k + 1).start()
        for s in range(streams):
            for p in range(low):
                acc[s][p] = acc[s][p] + recv[s][k][p].astype(F32)

    ag_step(0)

    squares = jnp.zeros((toks, 128), F32)
    for c in range(chunks):
        tok_copies[c].wait()

        def square(j, total, c=c):
            part = tok[:, pl.ds(pl.multiple_of(c * cw + j * 512, 512), 512)].astype(F32)
            part = part * part
            return total + (
                (part[:, :128] + part[:, 128:256]) + (part[:, 256:384] + part[:, 384:])
            )

        squares = lax.fori_loop(0, cw // 512, square, squares)
    rstd = lax.rsqrt(jnp.sum(squares, axis=1, keepdims=True) * (1.0 / width) + 1e-05)
    rstds[...] = jnp.broadcast_to(rstd, rstds.shape)
    gain_copy_in.wait()
    gains[...] = gain_ref[...].astype(F32)
    cot_copy.wait()

    ag_step(1)

    cot_t = cot_ref[...].T

    def weight_terms(flip):
        def body(q, carry):
            r = 2 * q + flip
            i = block_of(r)
            normed = tok[:, columns(i)].astype(F32) * across(rstds)
            hidden = (normed * gain_of(i)).astype(BF16)
            hid[:, columns(i)] = hidden
            terms = jnp.dot(cot_t, hidden, preferred_element_type=F32)
            for s in range(streams):
                part = terms[goff[s]: goff[s] + gsize[s]]
                if flip:
                    send[s][0][place(s, r) - count // 2] = part.astype(BF16)
                else:
                    acc[s][place(s, r)] = part
            return carry

        lax.fori_loop(0, count // 2, body, 0, unroll=4)

    weight_terms(1)
    for s in range(streams):
        rs_copy(s, 0).start()
    ag_step(2)
    weight_terms(0)
    rs_step(0)
    for k in range(3, bits):
        ag_step(k)

    def weight_pass(flip, begin, end, total):
        def body(q, total):
            r = 2 * q + flip
            i = block_of(r)
            block = jnp.concatenate([wbuf[s][place(s, r)] for s in range(streams)], axis=0)
            dhidden = lax.dot_general(
                cot_ref[...], block, (((1,), (1,)), ((), ())), preferred_element_type=F32
            )
            back[:, columns(i)] = dhidden * gain_of(i) * across(rstds)
            return total + jnp.dot(hid[:, columns(i)], block, preferred_element_type=F32)

        return lax.fori_loop(begin, end, body, total, unroll=4)

    half, quarter = count // 2, count // 4
    rs_step(1)
    total = weight_pass(0, 0, half, jnp.zeros((toks, heads), F32))
    rs_step(2)
    ag_step(bits)
    total = weight_pass(1, 0, quarter, total)
    for k in range(3, bits - 1):
        rs_step(k)
    total = weight_pass(1, quarter, half, total)

    def gain_copy(j):
        return pltpu.make_async_remote_copy(
            src_ref=gmine,
            dst_ref=gall.at[me],
            send_sem=g_send.at[j],
            recv_sem=g_recv.at[j],
            device_id=device((me + j) % count),
            device_id_type=MESH,
        )

    pieces = []
    for s in range(streams):
        rs_copy(s, bits - 1).wait_recv()
        pieces.append((acc[s][0] + recv[s][bits - 1][0].astype(F32)) * scale)
    grad = jnp.concatenate(pieces, axis=0).T
    product = grad * w_ref[...].astype(F32)
    sums = lax.dot_general(
        jnp.ones((8, heads), F32), product, (((1,), (1,)), ((), ())),
        precision=lax.Precision.HIGHEST, preferred_element_type=F32,
    )
    own = sums[:1] / gain_of(me)
    gmine[...] = own
    gall[me] = own

    def give(j, carry):
        gain_copy(j).start()
        return carry

    lax.fori_loop(1, count, give, 0)
    wg_ref[...] = grad
    keys_ref[...] = total.astype(BF16)
    outs = [
        pltpu.make_async_copy(wg_ref, wg_hbm, out_sem.at[0]),
        pltpu.make_async_copy(keys_ref, keys_hbm, out_sem.at[1]),
    ]
    for copy in outs:
        copy.start()
    inner = jnp.sum(total * cot_ref[...].astype(F32), axis=1, keepdims=True) * (1.0 / width)
    rowco[...] = rstds[...] * rstds[...] * inner

    def token_part(i, carry):
        tg_ref[:, columns(i)] = (
            back[:, columns(i)] - tok[:, columns(i)].astype(F32) * across(rowco)
        ).astype(BF16)
        return carry

    for g in range(chunks):
        lax.fori_loop(
            g * count // chunks, (g + 1) * count // chunks, token_part, 0, unroll=2
        )
        outs.append(
            pltpu.make_async_copy(
                tg_ref.at[:, pl.ds(g * cw, cw)], tg_hbm.at[:, pl.ds(g * cw, cw)],
                out_sem.at[3 + g],
            )
        )
        outs[-1].start()

    def taken(j, carry):
        gain_copy(j).wait_recv()
        gain_copy(j).wait_send()
        return carry

    lax.fori_loop(1, count, taken, 0)
    for b in range(count):
        for j in range(parts):
            gg_ref[b * parts + j: b * parts + j + 1, :] = gall[b, :, j * 128: (j + 1) * 128]
    outs.append(pltpu.make_async_copy(gg_ref, gg_hbm, out_sem.at[2]))
    outs[-1].start()
    for s in range(streams):
        for k in range(bits):
            ag_copy(s, k).wait_send()
            rs_copy(s, k).wait_send()
    for copy in outs:
        copy.wait()


def hand_out(*refs):
    sems = refs[-1]
    pairs = (len(refs) - 1) // 2
    copies = [
        pltpu.make_async_copy(refs[n], refs[pairs + n], sems.at[n]) for n in range(pairs)
    ]
    for copy in copies:
        copy.start()
    for copy in copies:
        copy.wait()


def fused(local_count, count, scale, tokens, norm_gain, key_weight, key_cotangent):
    rows, heads = key_weight.shape
    toks, width = tokens.shape
    bits = count.bit_length() - 1
    plan = stream_plan(bits)
    shares, _ = plan
    hbm = pl.BlockSpec(memory_space=pltpu.HBM)
    anywhere = pl.BlockSpec(memory_space=pl.ANY)
    stages = [
        pltpu.VMEM((count >> (k + 1), n * heads // 8, rows), BF16)
        for n in shares
        for k in range(bits)
    ]
    shapes = (
        jax.ShapeDtypeStruct((toks, heads), BF16),
        jax.ShapeDtypeStruct((toks, width), BF16),
        jax.ShapeDtypeStruct((rows, heads), F32),
        jax.ShapeDtypeStruct((width // 128, 128), F32),
    )
    results = pl.pallas_call(
        functools.partial(kernel, plan, local_count, scale),
        out_shape=shapes,
        in_specs=[hbm] * 4,
        out_specs=[anywhere] * 4,
        scratch_shapes=[pltpu.VMEM(shape.shape, shape.dtype) for shape in shapes]
        + [
            pltpu.VMEM((toks, width), BF16),
            pltpu.VMEM((width // 128, 128), BF16),
            pltpu.VMEM((rows, heads), BF16),
            pltpu.VMEM((toks, heads), BF16),
            pltpu.VMEM((toks, width), BF16),
            pltpu.VMEM((toks, width), F32),
            pltpu.VMEM((width // 128, 128), F32),
            pltpu.VMEM((toks, 128), F32),
            pltpu.VMEM((toks, 128), F32),
            pltpu.VMEM((1, rows), F32),
            pltpu.VMEM((count, 1, rows), F32),
        ]
        + [pltpu.VMEM((count, n * rows // 8, heads), BF16) for n in shares]
        + [pltpu.VMEM((count // 2, n * heads // 8, rows), F32) for n in shares]
        + stages
        + stages
        + [
            pltpu.SemaphoreType.DMA((4,)),
            pltpu.SemaphoreType.DMA((3,)),
            pltpu.SemaphoreType.DMA((7,)),
            pltpu.SemaphoreType.DMA((len(shares), bits)),
            pltpu.SemaphoreType.DMA((len(shares), bits)),
            pltpu.SemaphoreType.DMA((len(shares), bits)),
            pltpu.SemaphoreType.DMA((len(shares), bits)),
            pltpu.SemaphoreType.DMA((count,)),
            pltpu.SemaphoreType.DMA((count,)),
        ],
        compiler_params=pltpu.CompilerParams(
            collective_id=0, has_side_effects=True, vmem_limit_bytes=58 * 2**20
        ),
        cost_estimate=pl.CostEstimate(
            flops=6 * toks * width * heads, bytes_accessed=4 * toks * width, transcendentals=0
        ),
    )(tokens, norm_gain.reshape(width // 128, 128), key_weight, key_cotangent)
    keys, tg, wg, gg = pl.pallas_call(
        hand_out,
        out_shape=shapes,
        in_specs=[anywhere] * 4,
        out_specs=[hbm] * 4,
        scratch_shapes=[pltpu.SemaphoreType.DMA((4,))],
        compiler_params=pltpu.CompilerParams(vmem_limit_bytes=58 * 2**20),
        cost_estimate=pl.CostEstimate(
            flops=0, bytes_accessed=4 * toks * width, transcendentals=0
        ),
    )(*results)
    return keys, tg, wg, gg.reshape(width)


def plain(scale, tokens, norm_gain, key_weight, key_cotangent):
    gain_wide = norm_gain.astype(F32)
    wide = tokens.astype(F32)
    rstd = lax.rsqrt(jnp.mean(wide * wide, axis=1, keepdims=True) + 1e-05)
    normed = wide * rstd
    hidden = (normed * gain_wide).astype(BF16)
    whole = lax.all_gather(key_weight, ("node", "local"), axis=0, tiled=True)
    keys = jnp.dot(hidden, whole, preferred_element_type=F32).astype(BF16)
    dhidden = lax.dot_general(
        key_cotangent, whole, (((1,), (1,)), ((), ())), preferred_element_type=F32
    )
    dnormed = dhidden * gain_wide
    inner = jnp.mean(dnormed * normed, axis=1, keepdims=True)
    token_grad = (rstd * (dnormed - normed * inner)).astype(BF16)
    gain_grad = lax.psum(jnp.sum(dhidden * normed, axis=0) * scale, ("node", "local"))
    terms = lax.dot_general(
        hidden, key_cotangent, (((0,), (0,)), ((), ())), preferred_element_type=F32
    )
    weight_grad = lax.psum_scatter(
        terms * scale, ("node", "local"), scatter_dimension=0, tiled=True
    )
    return keys, token_grad, weight_grad, gain_grad


def solution(mesh):
    local_count = mesh.shape["local"]
    count = mesh.shape["node"] * local_count

    def local(tokens, norm_gain, key_weight, key_cotangent):
        scale = 1.0 / math.sqrt(tokens.shape[0] * count)
        if key_weight.shape[0] % 128 == 0 and count & (count - 1) == 0 and count >= 16:
            return fused(
                local_count, count, scale, tokens, norm_gain, key_weight, key_cotangent
            )
        return plain(scale, tokens, norm_gain, key_weight, key_cotangent)

    placed = P(("node", "local"), None)
    return jax.shard_map(
        local,
        mesh=mesh,
        in_specs=(placed, P(), placed, placed),
        out_specs=(placed, placed, placed, P()),
        check_vma=False,
    )
```

```python
import functools
import math

import jax
import jax.numpy as jnp
from jax import lax
from jax.experimental import pallas as pl
from jax.experimental.pallas import tpu as pltpu
from jax.sharding import PartitionSpec as P

MESH = pl.DeviceIdType.MESH
F32 = jnp.float32
BF16 = jnp.bfloat16


def stream_plan(bits):
    rest = list(range(1, bits))
    if bits == 5:
        return [3, 3, 2], [[0, 1, 2, 3, 4], [0, 2, 3, 4, 1], [0, 3, 4, 1, 2]]
    return [4, 4], [[0] + rest, [0] + rest[::-1]]


def gain_groups(bits):
    rest = list(range(1, bits))
    return [rest[max(0, n - 2): n] for n in range(len(rest), 0, -2)] + [[0]]


def kernel(
    plan, local_count, scale, tok_hbm, gain_hbm, w_hbm, cot_hbm,
    keys_hbm, tg_hbm, wg_hbm, gg_hbm,
    keys_ref, tg_ref, wg_ref, gg_ref, tok, gain_ref, w_ref, cot_ref, hid, back, gains, rstds, rowco, gall, *rest,
):
    shares, orders = plan
    bits = len(orders[0])
    count = 1 << bits
    streams = len(shares)
    rows, heads = w_ref.shape
    toks, width = tok.shape
    wsize = [n * rows // 8 for n in shares]
    woff = [sum(wsize[:s]) for s in range(streams)]
    gsize = [n * heads // 8 for n in shares]
    goff = [sum(gsize[:s]) for s in range(streams)]
    it = iter(rest)
    wbuf = [next(it) for _ in range(streams)]
    acc = [next(it) for _ in range(streams)]
    send = [[None] + [next(it) for _ in range(1, bits)] for _ in range(streams)]
    recv = [[None] + [next(it) for _ in range(1, bits)] for _ in range(streams)]
    (sent, came) = next(it), next(it)
    (
        tok_sem, in_sem, out_sem, ag_send, ag_recv, fw_send, fw_recv,
        pair_send, pair_recv, rs_send, rs_recv, g_send, g_recv,
    ) = list(it)

    me = lax.axis_index("node") * local_count + lax.axis_index("local")
    mine = [(me // (1 << k)) % 2 for k in range(bits)]

    def device(index):
        return (index // local_count, index % local_count)

    def partner(r):
        return device(block_of(r))

    def block_of(r):
        total = 0
        for k in range(bits):
            total = total + (1 << k) * ((mine[k] + r // (1 << k)) % 2)
        return total

    def place(s, r):
        total = 0
        for j, k in enumerate(orders[s]):
            total = total + (1 << (bits - 1 - j)) * ((r // (1 << k)) % 2)
        return total

    def at_place(s, p):
        return sum(((p >> (bits - 1 - j)) & 1) << k for j, k in enumerate(orders[s]))

    def columns(i):
        return pl.ds(pl.multiple_of(i * rows, rows), rows)

    parts = rows // 128

    def gain_of(i):
        return jnp.concatenate(
            [gains[pl.ds(i * parts + j, 1), :] for j in range(parts)], axis=1
        )

    def across(ref):
        return jnp.concatenate([ref[...]] * parts, axis=1)

    w_copy = pltpu.make_async_copy(w_hbm, w_ref, in_sem.at[0])
    cot_copy = pltpu.make_async_copy(cot_hbm, cot_ref, in_sem.at[1])
    gain_copy_in = pltpu.make_async_copy(gain_hbm, gain_ref, in_sem.at[2])
    chunks = tok_sem.shape[0]
    cw = width // chunks
    tok_copies = [
        pltpu.make_async_copy(
            tok_hbm.at[:, pl.ds(c * cw, cw)], tok.at[:, pl.ds(c * cw, cw)], tok_sem.at[c]
        )
        for c in range(chunks)
    ]
    for copy in [w_copy] + tok_copies + [cot_copy, gain_copy_in]:
        copy.start()

    barrier = pltpu.get_barrier_semaphore()

    groups = [high for high in gain_groups(bits)]
    friends = sorted({1 << k for k in range(bits)} | {sum(1 << k for k in g) for g in groups})
    for r in friends:
        pl.semaphore_signal(barrier, inc=1, device_id=partner(r), device_id_type=MESH)
    w_copy.wait()
    for s in range(streams):
        wbuf[s][0] = w_ref[pl.ds(woff[s], wsize[s]), :]
    pl.semaphore_wait(barrier, len(friends))

    half, quarter = count // 2, count // 4

    def ag_copy(s, k):
        size = 1 << k
        return pltpu.make_async_remote_copy(
            src_ref=wbuf[s].at[pl.ds(0, size)],
            dst_ref=wbuf[s].at[pl.ds(size, size)],
            send_sem=ag_send.at[s, k],
            recv_sem=ag_recv.at[s, k],
            device_id=partner(1 << orders[s][bits - 1 - k]),
            device_id_type=MESH,
        )

    def forward(s, k):
        start, size = (1 << k) // 2, max(1, (1 << k) // 2)
        return pltpu.make_async_remote_copy(
            src_ref=wbuf[s].at[pl.ds(start, size)],
            dst_ref=wbuf[s].at[pl.ds(half + start, size)],
            send_sem=fw_send.at[s, k],
            recv_sem=fw_recv.at[s, k],
            device_id=partner(1),
            device_id_type=MESH,
        )

    def ag_step(k):
        for s in range(streams):
            if k:
                ag_copy(s, k - 1).wait_recv()
            if k < bits - 1:
                ag_copy(s, k).start()
            forward(s, k).start()

    def pair_copy(q):
        return pltpu.make_async_remote_copy(
            src_ref=sent.at[q],
            dst_ref=came.at[q],
            send_sem=pair_send.at[q],
            recv_sem=pair_recv.at[q],
            device_id=partner(1),
            device_id_type=MESH,
        )

    def rs_copy(s, k, c):
        size = count >> (k + 1)
        low = size // 2
        span = pl.ds(0, 1) if size == 1 else pl.ds(low * c, low)
        return pltpu.make_async_remote_copy(
            src_ref=send[s][k].at[span],
            dst_ref=recv[s][k].at[span],
            send_sem=rs_send.at[s, k, c],
            recv_sem=rs_recv.at[s, k, c],
            device_id=partner(1 << orders[s][k]),
            device_id_type=MESH,
        )

    def halves(k):
        return (1, 0) if count >> (k + 1) > 1 else (0,)

    def incoming(s, k, p):
        if k:
            return recv[s][k][p].astype(F32)
        return came[at_place(s, p) // 2, goff[s]: goff[s] + gsize[s], :].astype(F32)

    def rs_step(k):
        low = count >> (k + 2)
        if k == 0:
            for q in range(half):
                pair_copy(q).wait_recv()
        for s in range(streams):
            if k:
                rs_copy(s, k, 1).wait_recv()
            for c in halves(k + 1):
                size = max(1, low // 2)
                for p in range(c * size, (c + 1) * size):
                    send[s][k + 1][p] = (
                        acc[s][low + p] + incoming(s, k, low + p)
                    ).astype(BF16)
                rs_copy(s, k + 1, c).start()
        for s in range(streams):
            if k:
                rs_copy(s, k, 0).wait_recv()
            for p in range(low):
                acc[s][p] = acc[s][p] + incoming(s, k, p)

    ag_step(0)

    squares = jnp.zeros((toks, 128), F32)
    for c in range(chunks):
        tok_copies[c].wait()

        def square(j, total, c=c):
            part = tok[:, pl.ds(pl.multiple_of(c * cw + j * 512, 512), 512)].astype(F32)
            part = part * part
            return total + (
                (part[:, :128] + part[:, 128:256]) + (part[:, 256:384] + part[:, 384:])
            )

        squares = lax.fori_loop(0, cw // 512, square, squares)
    rstd = lax.rsqrt(jnp.sum(squares, axis=1, keepdims=True) * (1.0 / width) + 1e-05)
    rstds[...] = jnp.broadcast_to(rstd, rstds.shape)
    gain_copy_in.wait()
    gains[...] = gain_ref[...].astype(F32)
    cot_copy.wait()

    ag_step(1)

    cot_t = cot_ref[...].T

    def weight_terms(flip, begin, end):
        def body(q, carry):
            r = 2 * q + flip
            i = block_of(r)
            normed = tok[:, columns(i)].astype(F32) * across(rstds)
            hidden = (normed * gain_of(i)).astype(BF16)
            hid[:, columns(i)] = hidden
            terms = jnp.dot(cot_t, hidden, preferred_element_type=F32)
            if flip:
                sent[q] = terms.astype(BF16)
                pair_copy(q).start()
            else:
                for s in range(streams):
                    acc[s][place(s, r)] = terms[goff[s]: goff[s] + gsize[s]]
            return carry

        lax.fori_loop(begin, end, body, 0, unroll=4)

    weight_terms(1, 0, quarter)
    ag_step(2)
    weight_terms(1, quarter, half)
    weight_terms(0, 0, quarter)
    for k in range(3, bits - 1):
        ag_step(k)
    weight_terms(0, quarter, half)
    rs_step(0)

    def weight_pass(flip, begin, end, total):
        def body(q, total):
            r = 2 * q + flip
            i = block_of(r)
            block = jnp.concatenate([wbuf[s][place(s, r)] for s in range(streams)], axis=0)
            dhidden = lax.dot_general(
                cot_ref[...], block, (((1,), (1,)), ((), ())), preferred_element_type=F32
            )
            back[:, columns(i)] = dhidden * gain_of(i) * across(rstds)
            return total + jnp.dot(hid[:, columns(i)], block, preferred_element_type=F32)

        return lax.fori_loop(begin, end, body, total, unroll=4)

    rs_step(1)
    ag_step(bits - 1)
    total = weight_pass(0, 0, half, jnp.zeros((toks, heads), F32))
    rs_step(2)
    for s in range(streams):
        for k in range(bits):
            forward(s, k).wait_recv()
    total = weight_pass(1, 0, quarter, total)
    for k in range(3, bits - 1):
        rs_step(k)
    total = weight_pass(1, quarter, half, total)

    sends, spans, ranks = [], [], [0]
    for g in groups:
        steps = [sum(1 << k for n, k in enumerate(g) if m >> n & 1) for m in range(1, 1 << len(g))]
        spans.append([(r, len(ranks) * (m + 1), len(ranks)) for m, r in enumerate(steps)])
        ranks = ranks + [x + r for r in steps for x in ranks]

    def gain_copies(phase):
        base = sum(len(span) for span in spans[:phase])
        return [
            pltpu.make_async_remote_copy(
                src_ref=gall.at[pl.ds(0, size)],
                dst_ref=gall.at[pl.ds(start, size)],
                send_sem=g_send.at[base + n],
                recv_sem=g_recv.at[base + n],
                device_id=partner(r),
                device_id_type=MESH,
            )
            for n, (r, start, size) in enumerate(spans[phase])
        ]

    def gain_step(phase):
        if phase:
            for copy in gain_copies(phase - 1):
                copy.wait_recv()
        if phase < len(groups):
            for copy in gain_copies(phase):
                copy.start()

    pieces = []
    for s in range(streams):
        rs_copy(s, bits - 1, 0).wait_recv()
        pieces.append((acc[s][0] + recv[s][bits - 1][0].astype(F32)) * scale)
    grad = jnp.concatenate(pieces, axis=0).T
    product = grad * w_ref[...].astype(F32)
    sums = lax.dot_general(
        jnp.ones((8, heads), F32), product, (((1,), (1,)), ((), ())),
        precision=lax.Precision.HIGHEST, preferred_element_type=F32,
    )
    own = sums[:1] / gain_of(me)
    gall[0] = own
    gain_step(0)

    wg_ref[...] = grad
    keys_ref[...] = total.astype(BF16)
    outs = [
        pltpu.make_async_copy(wg_ref, wg_hbm, out_sem.at[0]),
        pltpu.make_async_copy(keys_ref, keys_hbm, out_sem.at[1]),
    ]
    for copy in outs:
        copy.start()
    inner = jnp.sum(total * cot_ref[...].astype(F32), axis=1, keepdims=True) * (1.0 / width)
    rowco[...] = rstds[...] * rstds[...] * inner

    def token_part(i, carry):
        tg_ref[:, columns(i)] = (
            back[:, columns(i)] - tok[:, columns(i)].astype(F32) * across(rowco)
        ).astype(BF16)
        return carry

    for g in range(chunks):
        lax.fori_loop(
            g * count // chunks, (g + 1) * count // chunks, token_part, 0, unroll=2
        )
        outs.append(
            pltpu.make_async_copy(
                tg_ref.at[:, pl.ds(g * cw, cw)], tg_hbm.at[:, pl.ds(g * cw, cw)],
                out_sem.at[3 + g],
            )
        )
        outs[-1].start()
        if g % 2 and g < 2 * len(groups) - 2:
            gain_step(g // 2 + 1)
    for phase in range(chunks // 2 + 1, len(groups) + 1):
        gain_step(phase)
    for p, r in enumerate(ranks):
        i = block_of(r)
        for j in range(parts):
            gg_ref[pl.ds(i * parts + j, 1), :] = gall[p, :, j * 128: (j + 1) * 128]
    outs.append(pltpu.make_async_copy(gg_ref, gg_hbm, out_sem.at[2]))
    outs[-1].start()
    for s in range(streams):
        for k in range(bits):
            forward(s, k).wait_send()
            if k < bits - 1:
                ag_copy(s, k).wait_send()
            if k:
                for c in halves(k):
                    rs_copy(s, k, c).wait_send()
    for q in range(half):
        pair_copy(q).wait_send()
    for phase in range(len(groups)):
        for copy in gain_copies(phase):
            copy.wait_send()
    for copy in outs:
        copy.wait()


def hand_out(pieces, *refs):
    pairs = len(pieces)
    here, there, between, into, out = (
        refs[:pairs], refs[pairs: 2 * pairs], refs[2 * pairs: 3 * pairs], refs[-2], refs[-1]
    )
    cuts = []
    for n, parts in enumerate(pieces):
        rows = here[n].shape[0] // parts
        cuts += [(n, pl.ds(m * rows, rows)) for m in range(parts)]
    first = [
        pltpu.make_async_copy(here[n].at[cut], between[n].at[cut], into.at[c])
        for c, (n, cut) in enumerate(cuts)
    ]
    second = [
        pltpu.make_async_copy(between[n].at[cut], there[n].at[cut], out.at[c])
        for c, (n, cut) in enumerate(cuts)
    ]
    for copy in first:
        copy.start()
    for before, after in zip(first, second):
        before.wait()
        after.start()
    for copy in second:
        copy.wait()


def fused(local_count, count, scale, tokens, norm_gain, key_weight, key_cotangent):
    rows, heads = key_weight.shape
    toks, width = tokens.shape
    bits = count.bit_length() - 1
    plan = stream_plan(bits)
    shares, _ = plan
    hbm = pl.BlockSpec(memory_space=pltpu.HBM)
    anywhere = pl.BlockSpec(memory_space=pl.ANY)
    stages = [
        pltpu.VMEM((count >> (k + 1), n * heads // 8, rows), BF16)
        for n in shares
        for k in range(1, bits)
    ]
    pieces = [1, 8, 1, 1]
    shapes = (
        jax.ShapeDtypeStruct((toks, heads), BF16),
        jax.ShapeDtypeStruct((toks, width), BF16),
        jax.ShapeDtypeStruct((rows, heads), F32),
        jax.ShapeDtypeStruct((width // 128, 128), F32),
    )
    results = pl.pallas_call(
        functools.partial(kernel, plan, local_count, scale),
        out_shape=shapes,
        in_specs=[hbm] * 4,
        out_specs=[anywhere] * 4,
        scratch_shapes=[pltpu.VMEM(shape.shape, shape.dtype) for shape in shapes]
        + [
            pltpu.VMEM((toks, width), BF16),
            pltpu.VMEM((width // 128, 128), BF16),
            pltpu.VMEM((rows, heads), BF16),
            pltpu.VMEM((toks, heads), BF16),
            pltpu.VMEM((toks, width), BF16),
            pltpu.VMEM((toks, width), F32),
            pltpu.VMEM((width // 128, 128), F32),
            pltpu.VMEM((toks, 128), F32),
            pltpu.VMEM((toks, 128), F32),
            pltpu.VMEM((count, 1, rows), F32),
        ]
        + [pltpu.VMEM((count, n * rows // 8, heads), BF16) for n in shares]
        + [pltpu.VMEM((count // 2, n * heads // 8, rows), F32) for n in shares]
        + stages
        + stages
        + [pltpu.VMEM((count // 2, heads, rows), BF16)] * 2
        + [
            pltpu.SemaphoreType.DMA((4,)),
            pltpu.SemaphoreType.DMA((3,)),
            pltpu.SemaphoreType.DMA((7,)),
            pltpu.SemaphoreType.DMA((len(shares), bits)),
            pltpu.SemaphoreType.DMA((len(shares), bits)),
            pltpu.SemaphoreType.DMA((len(shares), bits)),
            pltpu.SemaphoreType.DMA((len(shares), bits)),
            pltpu.SemaphoreType.DMA((count // 2,)),
            pltpu.SemaphoreType.DMA((count // 2,)),
            pltpu.SemaphoreType.DMA((len(shares), bits, 2)),
            pltpu.SemaphoreType.DMA((len(shares), bits, 2)),
            pltpu.SemaphoreType.DMA((3 * bits,)),
            pltpu.SemaphoreType.DMA((3 * bits,)),
        ],
        compiler_params=pltpu.CompilerParams(
            collective_id=0, has_side_effects=True, vmem_limit_bytes=58 * 2**20
        ),
        cost_estimate=pl.CostEstimate(
            flops=6 * toks * width * heads, bytes_accessed=4 * toks * width, transcendentals=0
        ),
    )(tokens, norm_gain.reshape(width // 128, 128), key_weight, key_cotangent)
    keys, tg, wg, gg = pl.pallas_call(
        functools.partial(hand_out, pieces),
        out_shape=shapes,
        in_specs=[anywhere] * 4,
        out_specs=[hbm] * 4,
        scratch_shapes=[pltpu.VMEM(shape.shape, shape.dtype) for shape in shapes]
        + [pltpu.SemaphoreType.DMA((sum(pieces),))] * 2,
        compiler_params=pltpu.CompilerParams(vmem_limit_bytes=58 * 2**20),
        cost_estimate=pl.CostEstimate(
            flops=0, bytes_accessed=4 * toks * width, transcendentals=0
        ),
    )(*results)
    return keys, tg, wg, gg.reshape(width)


def plain(scale, tokens, norm_gain, key_weight, key_cotangent):
    gain_wide = norm_gain.astype(F32)
    wide = tokens.astype(F32)
    rstd = lax.rsqrt(jnp.mean(wide * wide, axis=1, keepdims=True) + 1e-05)
    normed = wide * rstd
    hidden = (normed * gain_wide).astype(BF16)
    whole = lax.all_gather(key_weight, ("node", "local"), axis=0, tiled=True)
    keys = jnp.dot(hidden, whole, preferred_element_type=F32).astype(BF16)
    dhidden = lax.dot_general(
        key_cotangent, whole, (((1,), (1,)), ((), ())), preferred_element_type=F32
    )
    dnormed = dhidden * gain_wide
    inner = jnp.mean(dnormed * normed, axis=1, keepdims=True)
    token_grad = (rstd * (dnormed - normed * inner)).astype(BF16)
    gain_grad = lax.psum(jnp.sum(dhidden * normed, axis=0) * scale, ("node", "local"))
    terms = lax.dot_general(
        hidden, key_cotangent, (((0,), (0,)), ((), ())), preferred_element_type=F32
    )
    weight_grad = lax.psum_scatter(
        terms * scale, ("node", "local"), scatter_dimension=0, tiled=True
    )
    return keys, token_grad, weight_grad, gain_grad


def solution(mesh):
    local_count = mesh.shape["local"]
    count = mesh.shape["node"] * local_count

    def local(tokens, norm_gain, key_weight, key_cotangent):
        scale = 1.0 / math.sqrt(tokens.shape[0] * count)
        if key_weight.shape[0] % 128 == 0 and count & (count - 1) == 0 and count >= 16:
            return fused(
                local_count, count, scale, tokens, norm_gain, key_weight, key_cotangent
            )
        return plain(scale, tokens, norm_gain, key_weight, key_cotangent)

    placed = P(("node", "local"), None)
    return jax.shard_map(
        local,
        mesh=mesh,
        in_specs=(placed, P(), placed, placed),
        out_specs=(placed, placed, placed, P()),
        check_vma=False,
    )
```

```python
import functools
import math

import jax
import jax.numpy as jnp
from jax import lax
from jax.experimental import pallas as pl
from jax.experimental.pallas import tpu as pltpu
from jax.sharding import PartitionSpec as P

MESH = pl.DeviceIdType.MESH
F32 = jnp.float32
BF16 = jnp.bfloat16


def stream_plan(bits):
    rest = list(range(1, bits))
    if bits == 5:
        return [3, 3, 2], [[0, 1, 2, 3, 4], [0, 2, 3, 4, 1], [0, 3, 4, 1, 2]]
    return [4, 4], [[0] + rest, [0] + rest[::-1]]


def gain_groups(bits):
    rest = list(range(1, bits))
    return [rest[max(0, n - 2): n] for n in range(len(rest), 0, -2)] + [[0]]


def kernel(
    plan, local_count, scale, tok_hbm, gain_hbm, w_hbm, cot_hbm,
    keys_hbm, tg_hbm, wg_hbm, gg_hbm,
    keys_ref, tg_ref, wg_ref, gg_ref, tok, gain_ref, w_ref, cot_ref, hid, back, gains, rstds, rowco, gall, *rest,
):
    shares, orders = plan
    bits = len(orders[0])
    count = 1 << bits
    streams = len(shares)
    rows, heads = w_ref.shape
    toks, width = tok.shape
    wsize = [n * rows // 8 for n in shares]
    woff = [sum(wsize[:s]) for s in range(streams)]
    gsize = [n * heads // 8 for n in shares]
    goff = [sum(gsize[:s]) for s in range(streams)]
    it = iter(rest)
    wbuf = [next(it) for _ in range(streams)]
    acc = [next(it) for _ in range(streams)]
    send = [[None] + [next(it) for _ in range(1, bits)] for _ in range(streams)]
    recv = [[None] + [next(it) for _ in range(1, bits)] for _ in range(streams)]
    (sent, came) = next(it), next(it)
    (
        tok_sem, in_sem, out_sem, ag_send, ag_recv, fw_send, fw_recv,
        pair_send, pair_recv, rs_send, rs_recv, g_send, g_recv,
    ) = list(it)

    me = lax.axis_index("node") * local_count + lax.axis_index("local")
    flips = [(1 << k) * (1 - 2 * ((me // (1 << k)) % 2)) for k in range(bits)]

    def device(index):
        return (index // local_count, index % local_count)

    def partner(r):
        return device(block_of(r))

    def block_of(r):
        total = me
        for k in range(bits):
            if r >> k & 1:
                total = total + flips[k]
        return total

    def place(s, r):
        return sum((r >> k & 1) << (bits - 1 - j) for j, k in enumerate(orders[s]))

    def at_place(s, p):
        return sum(((p >> (bits - 1 - j)) & 1) << k for j, k in enumerate(orders[s]))

    def columns(i):
        return pl.ds(pl.multiple_of(i * rows, rows), rows)

    parts = rows // 128

    def gain_of(i):
        return jnp.concatenate(
            [gains[pl.ds(i * parts + j, 1), :] for j in range(parts)], axis=1
        )

    def across(ref):
        return jnp.concatenate([ref[...]] * parts, axis=1)

    w_copy = pltpu.make_async_copy(w_hbm, w_ref, in_sem.at[0])
    cot_copy = pltpu.make_async_copy(cot_hbm, cot_ref, in_sem.at[1])
    gain_copy_in = pltpu.make_async_copy(gain_hbm, gain_ref, in_sem.at[2])
    chunks = tok_sem.shape[0]
    cw = width // chunks
    tok_copies = [
        pltpu.make_async_copy(
            tok_hbm.at[:, pl.ds(c * cw, cw)], tok.at[:, pl.ds(c * cw, cw)], tok_sem.at[c]
        )
        for c in range(chunks)
    ]
    for copy in [w_copy] + tok_copies + [cot_copy, gain_copy_in]:
        copy.start()

    barrier = pltpu.get_barrier_semaphore()

    groups = [high for high in gain_groups(bits)]
    friends = sorted({1 << k for k in range(bits)} | {sum(1 << k for k in g) for g in groups})
    for r in friends:
        pl.semaphore_signal(barrier, inc=1, device_id=partner(r), device_id_type=MESH)
    w_copy.wait()
    for s in range(streams):
        wbuf[s][0] = w_ref[pl.ds(woff[s], wsize[s]), :]
    pl.semaphore_wait(barrier, len(friends))

    half, quarter = count // 2, count // 4

    def ag_copy(s, k):
        size = 1 << k
        return pltpu.make_async_remote_copy(
            src_ref=wbuf[s].at[pl.ds(0, size)],
            dst_ref=wbuf[s].at[pl.ds(size, size)],
            send_sem=ag_send.at[s, k],
            recv_sem=ag_recv.at[s, k],
            device_id=partner(1 << orders[s][bits - 1 - k]),
            device_id_type=MESH,
        )

    def forward(s, k):
        start, size = (1 << k) // 2, max(1, (1 << k) // 2)
        return pltpu.make_async_remote_copy(
            src_ref=wbuf[s].at[pl.ds(start, size)],
            dst_ref=wbuf[s].at[pl.ds(half + start, size)],
            send_sem=fw_send.at[s, k],
            recv_sem=fw_recv.at[s, k],
            device_id=partner(1),
            device_id_type=MESH,
        )

    def ag_step(k):
        for s in range(streams):
            if k:
                ag_copy(s, k - 1).wait_recv()
            if k < bits - 1:
                ag_copy(s, k).start()
            forward(s, k).start()

    def pair_copy(q):
        return pltpu.make_async_remote_copy(
            src_ref=sent.at[q],
            dst_ref=came.at[q],
            send_sem=pair_send.at[q],
            recv_sem=pair_recv.at[q],
            device_id=partner(1),
            device_id_type=MESH,
        )

    def rs_copy(s, k, c):
        size = count >> (k + 1)
        low = size // 2
        span = pl.ds(0, 1) if size == 1 else pl.ds(low * c, low)
        return pltpu.make_async_remote_copy(
            src_ref=send[s][k].at[span],
            dst_ref=recv[s][k].at[span],
            send_sem=rs_send.at[s, k, c],
            recv_sem=rs_recv.at[s, k, c],
            device_id=partner(1 << orders[s][k]),
            device_id_type=MESH,
        )

    def halves(k):
        return (1, 0) if count >> (k + 1) > 1 else (0,)

    def incoming(s, k, p):
        if k:
            return recv[s][k][p].astype(F32)
        return came[at_place(s, p) // 2, goff[s]: goff[s] + gsize[s], :].astype(F32)

    def rs_step(k):
        low = count >> (k + 2)
        if k == 0:
            for q in range(half):
                pair_copy(q).wait_recv()
        for s in range(streams):
            if k:
                rs_copy(s, k, 1).wait_recv()
            for c in halves(k + 1):
                size = max(1, low // 2)
                for p in range(c * size, (c + 1) * size):
                    send[s][k + 1][p] = (
                        acc[s][low + p] + incoming(s, k, low + p)
                    ).astype(BF16)
                rs_copy(s, k + 1, c).start()
        for s in range(streams):
            if k:
                rs_copy(s, k, 0).wait_recv()
            for p in range(low):
                acc[s][p] = acc[s][p] + incoming(s, k, p)

    ag_step(0)

    squares = jnp.zeros((toks, 128), F32)
    for c in range(chunks):
        tok_copies[c].wait()

        def square(j, total, c=c):
            part = tok[:, pl.ds(pl.multiple_of(c * cw + j * 512, 512), 512)].astype(F32)
            part = part * part
            return total + (
                (part[:, :128] + part[:, 128:256]) + (part[:, 256:384] + part[:, 384:])
            )

        squares = lax.fori_loop(0, cw // 512, square, squares)
    rstd = lax.rsqrt(jnp.sum(squares, axis=1, keepdims=True) * (1.0 / width) + 1e-05)
    rstds[...] = jnp.broadcast_to(rstd, rstds.shape)
    gain_copy_in.wait()
    gains[...] = gain_ref[...].astype(F32)
    cot_copy.wait()

    ag_step(1)

    cot_t = cot_ref[...].T

    def weight_terms(flip, begin, end):
        for q in range(begin, end):
            r = 2 * q + flip
            i = block_of(r)
            normed = tok[:, columns(i)].astype(F32) * across(rstds)
            hidden = (normed * gain_of(i)).astype(BF16)
            hid[:, columns(i)] = hidden
            terms = jnp.dot(cot_t, hidden, preferred_element_type=F32)
            if flip:
                sent[q] = terms.astype(BF16)
                pair_copy(q).start()
            else:
                for s in range(streams):
                    acc[s][place(s, r)] = terms[goff[s]: goff[s] + gsize[s]]

    weight_terms(1, 0, quarter)
    ag_step(2)
    weight_terms(1, quarter, half)
    weight_terms(0, 0, quarter)
    for k in range(3, bits - 1):
        ag_step(k)
    weight_terms(0, quarter, half)
    rs_step(0)

    def weight_pass(flip, begin, end, total):
        for q in range(begin, end):
            r = 2 * q + flip
            i = block_of(r)
            block = jnp.concatenate([wbuf[s][place(s, r)] for s in range(streams)], axis=0)
            dhidden = lax.dot_general(
                cot_ref[...], block, (((1,), (1,)), ((), ())), preferred_element_type=F32
            )
            back[:, columns(i)] = dhidden * gain_of(i) * across(rstds)
            total = total + jnp.dot(hid[:, columns(i)], block, preferred_element_type=F32)
        return total

    rs_step(1)
    ag_step(bits - 1)
    total = weight_pass(0, 0, half, jnp.zeros((toks, heads), F32))
    rs_step(2)
    for s in range(streams):
        for k in range(bits):
            forward(s, k).wait_recv()
    total = weight_pass(1, 0, quarter, total)
    for k in range(3, bits - 1):
        rs_step(k)
    total = weight_pass(1, quarter, half, total)

    sends, spans, ranks = [], [], [0]
    for g in groups:
        steps = [sum(1 << k for n, k in enumerate(g) if m >> n & 1) for m in range(1, 1 << len(g))]
        spans.append([(r, len(ranks) * (m + 1), len(ranks)) for m, r in enumerate(steps)])
        ranks = ranks + [x + r for r in steps for x in ranks]

    def gain_copies(phase):
        base = sum(len(span) for span in spans[:phase])
        return [
            pltpu.make_async_remote_copy(
                src_ref=gall.at[pl.ds(0, size)],
                dst_ref=gall.at[pl.ds(start, size)],
                send_sem=g_send.at[base + n],
                recv_sem=g_recv.at[base + n],
                device_id=partner(r),
                device_id_type=MESH,
            )
            for n, (r, start, size) in enumerate(spans[phase])
        ]

    def gain_step(phase):
        if phase:
            for copy in gain_copies(phase - 1):
                copy.wait_recv()
        if phase < len(groups):
            for copy in gain_copies(phase):
                copy.start()

    pieces = []
    for s in range(streams):
        rs_copy(s, bits - 1, 0).wait_recv()
        pieces.append((acc[s][0] + recv[s][bits - 1][0].astype(F32)) * scale)
    grad = jnp.concatenate(pieces, axis=0).T
    product = grad * w_ref[...].astype(F32)
    sums = lax.dot_general(
        jnp.ones((8, heads), F32), product, (((1,), (1,)), ((), ())),
        precision=lax.Precision.HIGHEST, preferred_element_type=F32,
    )
    own = sums[:1] / gain_of(me)
    gall[0] = own
    gain_step(0)

    wg_ref[...] = grad
    keys_ref[...] = total.astype(BF16)
    outs = [
        pltpu.make_async_copy(wg_ref, wg_hbm, out_sem.at[0]),
        pltpu.make_async_copy(keys_ref, keys_hbm, out_sem.at[1]),
    ]
    for copy in outs:
        copy.start()
    inner = jnp.sum(total * cot_ref[...].astype(F32), axis=1, keepdims=True) * (1.0 / width)
    rowco[...] = rstds[...] * rstds[...] * inner

    def token_part(i, carry):
        tg_ref[:, columns(i)] = (
            back[:, columns(i)] - tok[:, columns(i)].astype(F32) * across(rowco)
        ).astype(BF16)
        return carry

    for g in range(chunks):
        lax.fori_loop(
            g * count // chunks, (g + 1) * count // chunks, token_part, 0, unroll=2
        )
        outs.append(
            pltpu.make_async_copy(
                tg_ref.at[:, pl.ds(g * cw, cw)], tg_hbm.at[:, pl.ds(g * cw, cw)],
                out_sem.at[3 + g],
            )
        )
        outs[-1].start()
        if g % 2 and g < 2 * len(groups) - 2:
            gain_step(g // 2 + 1)
    for phase in range(chunks // 2 + 1, len(groups) + 1):
        gain_step(phase)
    for p, r in enumerate(ranks):
        i = block_of(r)
        for j in range(parts):
            gg_ref[pl.ds(i * parts + j, 1), :] = gall[p, :, j * 128: (j + 1) * 128]
    outs.append(pltpu.make_async_copy(gg_ref, gg_hbm, out_sem.at[2]))
    outs[-1].start()
    for s in range(streams):
        for k in range(bits):
            forward(s, k).wait_send()
            if k < bits - 1:
                ag_copy(s, k).wait_send()
            if k:
                for c in halves(k):
                    rs_copy(s, k, c).wait_send()
    for q in range(half):
        pair_copy(q).wait_send()
    for phase in range(len(groups)):
        for copy in gain_copies(phase):
            copy.wait_send()
    for copy in outs:
        copy.wait()


def hand_out(pieces, *refs):
    pairs = len(pieces)
    here, there, between, into, out = (
        refs[:pairs], refs[pairs: 2 * pairs], refs[2 * pairs: 3 * pairs], refs[-2], refs[-1]
    )
    cuts = []
    for n, parts in enumerate(pieces):
        rows = here[n].shape[0] // parts
        cuts += [(n, pl.ds(m * rows, rows)) for m in range(parts)]
    first = [
        pltpu.make_async_copy(here[n].at[cut], between[n].at[cut], into.at[c])
        for c, (n, cut) in enumerate(cuts)
    ]
    second = [
        pltpu.make_async_copy(between[n].at[cut], there[n].at[cut], out.at[c])
        for c, (n, cut) in enumerate(cuts)
    ]
    for copy in first:
        copy.start()
    for before, after in zip(first, second):
        before.wait()
        after.start()
    for copy in second:
        copy.wait()


def fused(local_count, count, scale, tokens, norm_gain, key_weight, key_cotangent):
    rows, heads = key_weight.shape
    toks, width = tokens.shape
    bits = count.bit_length() - 1
    plan = stream_plan(bits)
    shares, _ = plan
    hbm = pl.BlockSpec(memory_space=pltpu.HBM)
    anywhere = pl.BlockSpec(memory_space=pl.ANY)
    stages = [
        pltpu.VMEM((count >> (k + 1), n * heads // 8, rows), BF16)
        for n in shares
        for k in range(1, bits)
    ]
    pieces = [1, 8, 1, 1]
    shapes = (
        jax.ShapeDtypeStruct((toks, heads), BF16),
        jax.ShapeDtypeStruct((toks, width), BF16),
        jax.ShapeDtypeStruct((rows, heads), F32),
        jax.ShapeDtypeStruct((width // 128, 128), F32),
    )
    results = pl.pallas_call(
        functools.partial(kernel, plan, local_count, scale),
        out_shape=shapes,
        in_specs=[hbm] * 4,
        out_specs=[anywhere] * 4,
        scratch_shapes=[pltpu.VMEM(shape.shape, shape.dtype) for shape in shapes]
        + [
            pltpu.VMEM((toks, width), BF16),
            pltpu.VMEM((width // 128, 128), BF16),
            pltpu.VMEM((rows, heads), BF16),
            pltpu.VMEM((toks, heads), BF16),
            pltpu.VMEM((toks, width), BF16),
            pltpu.VMEM((toks, width), F32),
            pltpu.VMEM((width // 128, 128), F32),
            pltpu.VMEM((toks, 128), F32),
            pltpu.VMEM((toks, 128), F32),
            pltpu.VMEM((count, 1, rows), F32),
        ]
        + [pltpu.VMEM((count, n * rows // 8, heads), BF16) for n in shares]
        + [pltpu.VMEM((count // 2, n * heads // 8, rows), F32) for n in shares]
        + stages
        + stages
        + [pltpu.VMEM((count // 2, heads, rows), BF16)] * 2
        + [
            pltpu.SemaphoreType.DMA((4,)),
            pltpu.SemaphoreType.DMA((3,)),
            pltpu.SemaphoreType.DMA((7,)),
            pltpu.SemaphoreType.DMA((len(shares), bits)),
            pltpu.SemaphoreType.DMA((len(shares), bits)),
            pltpu.SemaphoreType.DMA((len(shares), bits)),
            pltpu.SemaphoreType.DMA((len(shares), bits)),
            pltpu.SemaphoreType.DMA((count // 2,)),
            pltpu.SemaphoreType.DMA((count // 2,)),
            pltpu.SemaphoreType.DMA((len(shares), bits, 2)),
            pltpu.SemaphoreType.DMA((len(shares), bits, 2)),
            pltpu.SemaphoreType.DMA((3 * bits,)),
            pltpu.SemaphoreType.DMA((3 * bits,)),
        ],
        compiler_params=pltpu.CompilerParams(
            collective_id=0, has_side_effects=True, vmem_limit_bytes=58 * 2**20
        ),
        cost_estimate=pl.CostEstimate(
            flops=6 * toks * width * heads, bytes_accessed=4 * toks * width, transcendentals=0
        ),
    )(tokens, norm_gain.reshape(width // 128, 128), key_weight, key_cotangent)
    keys, tg, wg, gg = pl.pallas_call(
        functools.partial(hand_out, pieces),
        out_shape=shapes,
        in_specs=[anywhere] * 4,
        out_specs=[hbm] * 4,
        scratch_shapes=[pltpu.VMEM(shape.shape, shape.dtype) for shape in shapes]
        + [pltpu.SemaphoreType.DMA((sum(pieces),))] * 2,
        compiler_params=pltpu.CompilerParams(vmem_limit_bytes=58 * 2**20),
        cost_estimate=pl.CostEstimate(
            flops=0, bytes_accessed=4 * toks * width, transcendentals=0
        ),
    )(*results)
    return keys, tg, wg, gg.reshape(width)


def plain(scale, tokens, norm_gain, key_weight, key_cotangent):
    gain_wide = norm_gain.astype(F32)
    wide = tokens.astype(F32)
    rstd = lax.rsqrt(jnp.mean(wide * wide, axis=1, keepdims=True) + 1e-05)
    normed = wide * rstd
    hidden = (normed * gain_wide).astype(BF16)
    whole = lax.all_gather(key_weight, ("node", "local"), axis=0, tiled=True)
    keys = jnp.dot(hidden, whole, preferred_element_type=F32).astype(BF16)
    dhidden = lax.dot_general(
        key_cotangent, whole, (((1,), (1,)), ((), ())), preferred_element_type=F32
    )
    dnormed = dhidden * gain_wide
    inner = jnp.mean(dnormed * normed, axis=1, keepdims=True)
    token_grad = (rstd * (dnormed - normed * inner)).astype(BF16)
    gain_grad = lax.psum(jnp.sum(dhidden * normed, axis=0) * scale, ("node", "local"))
    terms = lax.dot_general(
        hidden, key_cotangent, (((0,), (0,)), ((), ())), preferred_element_type=F32
    )
    weight_grad = lax.psum_scatter(
        terms * scale, ("node", "local"), scatter_dimension=0, tiled=True
    )
    return keys, token_grad, weight_grad, gain_grad


def solution(mesh):
    local_count = mesh.shape["local"]
    count = mesh.shape["node"] * local_count

    def local(tokens, norm_gain, key_weight, key_cotangent):
        scale = 1.0 / math.sqrt(tokens.shape[0] * count)
        if key_weight.shape[0] % 128 == 0 and count & (count - 1) == 0 and count >= 16:
            return fused(
                local_count, count, scale, tokens, norm_gain, key_weight, key_cotangent
            )
        return plain(scale, tokens, norm_gain, key_weight, key_cotangent)

    placed = P(("node", "local"), None)
    return jax.shard_map(
        local,
        mesh=mesh,
        in_specs=(placed, P(), placed, placed),
        out_specs=(placed, placed, placed, P()),
        check_vma=False,
    )
```

```python
import functools
import math

import jax
import jax.numpy as jnp
from jax import lax
from jax.experimental import pallas as pl
from jax.experimental.pallas import tpu as pltpu
from jax.sharding import PartitionSpec as P

MESH = pl.DeviceIdType.MESH
F32 = jnp.float32
BF16 = jnp.bfloat16


def stream_plan(bits):
    rest = list(range(1, bits))
    if bits == 5:
        return [3, 3, 2], [[0, 1, 2, 3, 4], [0, 2, 1, 3, 4], [0, 3, 4, 1, 2]]
    return [4, 4], [[0] + rest, [0] + rest[::-1]]


def gain_groups(bits):
    return [list(range(1, bits)), [0]]


def masks(group):
    return [
        sum(1 << k for n, k in enumerate(group) if m >> n & 1) for m in range(1, 1 << len(group))
    ]


def kernel(
    plan, local_count, scale, tok_hbm, gain_hbm, w_hbm, cot_hbm,
    keys_hbm, tg_hbm, wg_hbm, gg_hbm,
    keys_ref, tg_ref, wg_ref, gg_ref, tok, gain_ref, w_ref, cot_ref, hid, back, gains, rstds, rowco, gall, *rest,
):
    shares, orders = plan
    bits = len(orders[0])
    count = 1 << bits
    streams = len(shares)
    rows, heads = w_ref.shape
    toks, width = tok.shape
    wsize = [n * rows // 8 for n in shares]
    woff = [sum(wsize[:s]) for s in range(streams)]
    gsize = [n * heads // 8 for n in shares]
    goff = [sum(gsize[:s]) for s in range(streams)]
    it = iter(rest)
    wbuf = [next(it) for _ in range(streams)]
    acc = [next(it) for _ in range(streams)]
    send = [[None] + [next(it) for _ in range(1, bits)] for _ in range(streams)]
    recv = [[None] + [next(it) for _ in range(1, bits)] for _ in range(streams)]
    (sent, came) = next(it), next(it)
    (
        tok_sem, in_sem, out_sem, ag_send, ag_recv, fw_send, fw_recv,
        pair_send, pair_recv, rs_send, rs_recv, g_send, g_recv,
    ) = list(it)

    me = lax.axis_index("node") * local_count + lax.axis_index("local")
    flips = [(1 << k) * (1 - 2 * ((me // (1 << k)) % 2)) for k in range(bits)]

    def device(index):
        return (index // local_count, index % local_count)

    def partner(r):
        return device(block_of(r))

    def block_of(r):
        total = me
        for k in range(bits):
            if r >> k & 1:
                total = total + flips[k]
        return total

    def place(s, r):
        return sum((r >> k & 1) << (bits - 1 - j) for j, k in enumerate(orders[s]))

    def at_place(s, p):
        return sum(((p >> (bits - 1 - j)) & 1) << k for j, k in enumerate(orders[s]))

    def columns(i):
        return pl.ds(pl.multiple_of(i * rows, rows), rows)

    parts = rows // 128

    def gain_of(i):
        return jnp.concatenate(
            [gains[pl.ds(i * parts + j, 1), :] for j in range(parts)], axis=1
        )

    def across(ref):
        return jnp.concatenate([ref[...]] * parts, axis=1)

    w_copy = pltpu.make_async_copy(w_hbm, w_ref, in_sem.at[0])
    cot_copy = pltpu.make_async_copy(cot_hbm, cot_ref, in_sem.at[1])
    gain_copy_in = pltpu.make_async_copy(gain_hbm, gain_ref, in_sem.at[2])
    chunks = tok_sem.shape[0]
    cw = width // chunks
    tok_copies = [
        pltpu.make_async_copy(
            tok_hbm.at[:, pl.ds(c * cw, cw)], tok.at[:, pl.ds(c * cw, cw)], tok_sem.at[c]
        )
        for c in range(chunks)
    ]
    for copy in [w_copy] + tok_copies + [cot_copy, gain_copy_in]:
        copy.start()

    barrier = pltpu.get_barrier_semaphore()

    groups = gain_groups(bits)
    friends = sorted({r for g in groups for r in masks(g)})
    for r in friends:
        pl.semaphore_signal(barrier, inc=1, device_id=partner(r), device_id_type=MESH)
    w_copy.wait()
    for s in range(streams):
        wbuf[s][0] = w_ref[pl.ds(woff[s], wsize[s]), :]
    pl.semaphore_wait(barrier, len(friends))

    half, quarter = count // 2, count // 4

    def ag_copy(s, k):
        size = 1 << k
        return pltpu.make_async_remote_copy(
            src_ref=wbuf[s].at[pl.ds(0, size)],
            dst_ref=wbuf[s].at[pl.ds(size, size)],
            send_sem=ag_send.at[s, k],
            recv_sem=ag_recv.at[s, k],
            device_id=partner(1 << orders[s][bits - 1 - k]),
            device_id_type=MESH,
        )

    def forward(s, k):
        start, size = (1 << k) // 2, max(1, (1 << k) // 2)
        return pltpu.make_async_remote_copy(
            src_ref=wbuf[s].at[pl.ds(start, size)],
            dst_ref=wbuf[s].at[pl.ds(half + start, size)],
            send_sem=fw_send.at[s, k],
            recv_sem=fw_recv.at[s, k],
            device_id=partner(1),
            device_id_type=MESH,
        )

    def ag_step(k):
        for s in range(streams):
            if k:
                ag_copy(s, k - 1).wait_recv()
            if k < bits - 1:
                ag_copy(s, k).start()
            forward(s, k).start()

    def pair_copy(q):
        return pltpu.make_async_remote_copy(
            src_ref=sent.at[q],
            dst_ref=came.at[q],
            send_sem=pair_send.at[q],
            recv_sem=pair_recv.at[q],
            device_id=partner(1),
            device_id_type=MESH,
        )

    def rs_copy(s, k, c):
        size = count >> (k + 1)
        low = size // 2
        span = pl.ds(0, 1) if size == 1 else pl.ds(low * c, low)
        return pltpu.make_async_remote_copy(
            src_ref=send[s][k].at[span],
            dst_ref=recv[s][k].at[span],
            send_sem=rs_send.at[s, k, c],
            recv_sem=rs_recv.at[s, k, c],
            device_id=partner(1 << orders[s][k]),
            device_id_type=MESH,
        )

    def halves(k):
        return (1, 0) if count >> (k + 1) > 1 else (0,)

    def incoming(s, k, p):
        if k:
            return recv[s][k][p].astype(F32)
        return came[at_place(s, p) // 2, goff[s]: goff[s] + gsize[s], :].astype(F32)

    def rs_step(k):
        low = count >> (k + 2)
        if k == 0:
            for q in range(half):
                pair_copy(q).wait_recv()
        for s in range(streams):
            if k:
                rs_copy(s, k, 1).wait_recv()
            for c in halves(k + 1):
                size = max(1, low // 2)
                for p in range(c * size, (c + 1) * size):
                    send[s][k + 1][p] = (
                        acc[s][low + p] + incoming(s, k, low + p)
                    ).astype(BF16)
                rs_copy(s, k + 1, c).start()
        for s in range(streams):
            if k:
                rs_copy(s, k, 0).wait_recv()
            for p in range(low):
                acc[s][p] = acc[s][p] + incoming(s, k, p)

    ag_step(0)

    squares = jnp.zeros((toks, 128), F32)
    for c in range(chunks):
        tok_copies[c].wait()

        def square(j, total, c=c):
            part = tok[:, pl.ds(pl.multiple_of(c * cw + j * 512, 512), 512)].astype(F32)
            part = part * part
            return total + (
                (part[:, :128] + part[:, 128:256]) + (part[:, 256:384] + part[:, 384:])
            )

        squares = lax.fori_loop(0, cw // 512, square, squares)
    rstd = lax.rsqrt(jnp.sum(squares, axis=1, keepdims=True) * (1.0 / width) + 1e-05)
    rstds[...] = jnp.broadcast_to(rstd, rstds.shape)
    gain_copy_in.wait()
    gains[...] = gain_ref[...].astype(F32)
    cot_copy.wait()

    ag_step(1)

    cot_t = cot_ref[...].T

    def weight_terms(flip, begin, end):
        for q in range(begin, end):
            r = 2 * q + flip
            i = block_of(r)
            normed = tok[:, columns(i)].astype(F32) * across(rstds)
            hidden = (normed * gain_of(i)).astype(BF16)
            hid[:, columns(i)] = hidden
            terms = jnp.dot(cot_t, hidden, preferred_element_type=F32)
            if flip:
                sent[q] = terms.astype(BF16)
                pair_copy(q).start()
            else:
                for s in range(streams):
                    acc[s][place(s, r)] = terms[goff[s]: goff[s] + gsize[s]]

    weight_terms(1, 0, quarter)
    ag_step(2)
    weight_terms(1, quarter, half)
    weight_terms(0, 0, quarter)
    for k in range(3, bits - 1):
        ag_step(k)
    weight_terms(0, quarter, half)
    rs_step(0)

    def weight_pass(flip, begin, end, total):
        for q in range(begin, end):
            r = 2 * q + flip
            i = block_of(r)
            block = jnp.concatenate([wbuf[s][place(s, r)] for s in range(streams)], axis=0)
            dhidden = lax.dot_general(
                cot_ref[...], block, (((1,), (1,)), ((), ())), preferred_element_type=F32
            )
            back[:, columns(i)] = dhidden * gain_of(i) * across(rstds)
            total = total + jnp.dot(hid[:, columns(i)], block, preferred_element_type=F32)
        return total

    rs_step(1)
    ag_step(bits - 1)
    total = weight_pass(0, 0, half, jnp.zeros((toks, heads), F32))
    rs_step(2)
    for s in range(streams):
        for k in range(bits):
            forward(s, k).wait_recv()
    total = weight_pass(1, 0, quarter, total)
    for k in range(3, bits - 1):
        rs_step(k)
    total = weight_pass(1, quarter, half, total)

    sends, spans, ranks = [], [], [0]
    for g in groups:
        steps = masks(g)
        spans.append([(r, len(ranks) * (m + 1), len(ranks)) for m, r in enumerate(steps)])
        ranks = ranks + [x + r for r in steps for x in ranks]

    def gain_copies(phase):
        base = sum(len(span) for span in spans[:phase])
        return [
            pltpu.make_async_remote_copy(
                src_ref=gall.at[pl.ds(0, size)],
                dst_ref=gall.at[pl.ds(start, size)],
                send_sem=g_send.at[base + n],
                recv_sem=g_recv.at[base + n],
                device_id=partner(r),
                device_id_type=MESH,
            )
            for n, (r, start, size) in enumerate(spans[phase])
        ]

    def gain_step(phase):
        if phase:
            for copy in gain_copies(phase - 1):
                copy.wait_recv()
        if phase < len(groups):
            for copy in gain_copies(phase):
                copy.start()

    pieces = []
    for s in range(streams):
        rs_copy(s, bits - 1, 0).wait_recv()
        pieces.append((acc[s][0] + recv[s][bits - 1][0].astype(F32)) * scale)
    grad = jnp.concatenate(pieces, axis=0).T
    product = grad * w_ref[...].astype(F32)
    sums = lax.dot_general(
        jnp.ones((8, heads), F32), product, (((1,), (1,)), ((), ())),
        precision=lax.Precision.HIGHEST, preferred_element_type=F32,
    )
    own = sums[:1] / gain_of(me)
    gall[0] = own
    gain_step(0)

    wg_ref[...] = grad
    keys_ref[...] = total.astype(BF16)
    outs = [
        pltpu.make_async_copy(wg_ref, wg_hbm, out_sem.at[0]),
        pltpu.make_async_copy(keys_ref, keys_hbm, out_sem.at[1]),
    ]
    for copy in outs:
        copy.start()
    inner = jnp.sum(total * cot_ref[...].astype(F32), axis=1, keepdims=True) * (1.0 / width)
    rowco[...] = rstds[...] * rstds[...] * inner

    def token_part(i, carry):
        tg_ref[:, columns(i)] = (
            back[:, columns(i)] - tok[:, columns(i)].astype(F32) * across(rowco)
        ).astype(BF16)
        return carry

    for g in range(chunks):
        lax.fori_loop(
            g * count // chunks, (g + 1) * count // chunks, token_part, 0, unroll=2
        )
        outs.append(
            pltpu.make_async_copy(
                tg_ref.at[:, pl.ds(g * cw, cw)], tg_hbm.at[:, pl.ds(g * cw, cw)],
                out_sem.at[3 + g],
            )
        )
        outs[-1].start()
        if g == chunks // 2:
            gain_step(1)
    for phase in range(2, len(groups) + 1):
        gain_step(phase)
    for p, r in enumerate(ranks):
        i = block_of(r)
        for j in range(parts):
            gg_ref[pl.ds(i * parts + j, 1), :] = gall[p, :, j * 128: (j + 1) * 128]
    outs.append(pltpu.make_async_copy(gg_ref, gg_hbm, out_sem.at[2]))
    outs[-1].start()
    for s in range(streams):
        for k in range(bits):
            forward(s, k).wait_send()
            if k < bits - 1:
                ag_copy(s, k).wait_send()
            if k:
                for c in halves(k):
                    rs_copy(s, k, c).wait_send()
    for q in range(half):
        pair_copy(q).wait_send()
    for phase in range(len(groups)):
        for copy in gain_copies(phase):
            copy.wait_send()
    for copy in outs:
        copy.wait()


def hand_out(pieces, *refs):
    pairs = len(pieces)
    here, there, between, into, out = (
        refs[:pairs], refs[pairs: 2 * pairs], refs[2 * pairs: 3 * pairs], refs[-2], refs[-1]
    )
    cuts = []
    for n, parts in enumerate(pieces):
        rows = here[n].shape[0] // parts
        cuts += [(n, pl.ds(m * rows, rows)) for m in range(parts)]
    first = [
        pltpu.make_async_copy(here[n].at[cut], between[n].at[cut], into.at[c])
        for c, (n, cut) in enumerate(cuts)
    ]
    second = [
        pltpu.make_async_copy(between[n].at[cut], there[n].at[cut], out.at[c])
        for c, (n, cut) in enumerate(cuts)
    ]
    for copy in first:
        copy.start()
    for before, after in zip(first, second):
        before.wait()
        after.start()
    for copy in second:
        copy.wait()


def fused(local_count, count, scale, tokens, norm_gain, key_weight, key_cotangent):
    rows, heads = key_weight.shape
    toks, width = tokens.shape
    bits = count.bit_length() - 1
    plan = stream_plan(bits)
    shares, _ = plan
    hbm = pl.BlockSpec(memory_space=pltpu.HBM)
    anywhere = pl.BlockSpec(memory_space=pl.ANY)
    stages = [
        pltpu.VMEM((count >> (k + 1), n * heads // 8, rows), BF16)
        for n in shares
        for k in range(1, bits)
    ]
    pieces = [1, 8, 1, 1]
    shapes = (
        jax.ShapeDtypeStruct((toks, heads), BF16),
        jax.ShapeDtypeStruct((toks, width), BF16),
        jax.ShapeDtypeStruct((rows, heads), F32),
        jax.ShapeDtypeStruct((width // 128, 128), F32),
    )
    results = pl.pallas_call(
        functools.partial(kernel, plan, local_count, scale),
        out_shape=shapes,
        in_specs=[hbm] * 4,
        out_specs=[anywhere] * 4,
        scratch_shapes=[pltpu.VMEM(shape.shape, shape.dtype) for shape in shapes]
        + [
            pltpu.VMEM((toks, width), BF16),
            pltpu.VMEM((width // 128, 128), BF16),
            pltpu.VMEM((rows, heads), BF16),
            pltpu.VMEM((toks, heads), BF16),
            pltpu.VMEM((toks, width), BF16),
            pltpu.VMEM((toks, width), F32),
            pltpu.VMEM((width // 128, 128), F32),
            pltpu.VMEM((toks, 128), F32),
            pltpu.VMEM((toks, 128), F32),
            pltpu.VMEM((count, 1, rows), F32),
        ]
        + [pltpu.VMEM((count, n * rows // 8, heads), BF16) for n in shares]
        + [pltpu.VMEM((count // 2, n * heads // 8, rows), F32) for n in shares]
        + stages
        + stages
        + [pltpu.VMEM((count // 2, heads, rows), BF16)] * 2
        + [
            pltpu.SemaphoreType.DMA((4,)),
            pltpu.SemaphoreType.DMA((3,)),
            pltpu.SemaphoreType.DMA((7,)),
            pltpu.SemaphoreType.DMA((len(shares), bits)),
            pltpu.SemaphoreType.DMA((len(shares), bits)),
            pltpu.SemaphoreType.DMA((len(shares), bits)),
            pltpu.SemaphoreType.DMA((len(shares), bits)),
            pltpu.SemaphoreType.DMA((count // 2,)),
            pltpu.SemaphoreType.DMA((count // 2,)),
            pltpu.SemaphoreType.DMA((len(shares), bits, 2)),
            pltpu.SemaphoreType.DMA((len(shares), bits, 2)),
            pltpu.SemaphoreType.DMA((count // 2,)),
            pltpu.SemaphoreType.DMA((count // 2,)),
        ],
        compiler_params=pltpu.CompilerParams(
            collective_id=0, has_side_effects=True, vmem_limit_bytes=58 * 2**20
        ),
        cost_estimate=pl.CostEstimate(
            flops=6 * toks * width * heads, bytes_accessed=4 * toks * width, transcendentals=0
        ),
    )(tokens, norm_gain.reshape(width // 128, 128), key_weight, key_cotangent)
    keys, tg, wg, gg = pl.pallas_call(
        functools.partial(hand_out, pieces),
        out_shape=shapes,
        in_specs=[anywhere] * 4,
        out_specs=[hbm] * 4,
        scratch_shapes=[pltpu.VMEM(shape.shape, shape.dtype) for shape in shapes]
        + [pltpu.SemaphoreType.DMA((sum(pieces),))] * 2,
        compiler_params=pltpu.CompilerParams(vmem_limit_bytes=58 * 2**20),
        cost_estimate=pl.CostEstimate(
            flops=0, bytes_accessed=4 * toks * width, transcendentals=0
        ),
    )(*results)
    return keys, tg, wg, gg.reshape(width)


def plain(scale, tokens, norm_gain, key_weight, key_cotangent):
    gain_wide = norm_gain.astype(F32)
    wide = tokens.astype(F32)
    rstd = lax.rsqrt(jnp.mean(wide * wide, axis=1, keepdims=True) + 1e-05)
    normed = wide * rstd
    hidden = (normed * gain_wide).astype(BF16)
    whole = lax.all_gather(key_weight, ("node", "local"), axis=0, tiled=True)
    keys = jnp.dot(hidden, whole, preferred_element_type=F32).astype(BF16)
    dhidden = lax.dot_general(
        key_cotangent, whole, (((1,), (1,)), ((), ())), preferred_element_type=F32
    )
    dnormed = dhidden * gain_wide
    inner = jnp.mean(dnormed * normed, axis=1, keepdims=True)
    token_grad = (rstd * (dnormed - normed * inner)).astype(BF16)
    gain_grad = lax.psum(jnp.sum(dhidden * normed, axis=0) * scale, ("node", "local"))
    terms = lax.dot_general(
        hidden, key_cotangent, (((0,), (0,)), ((), ())), preferred_element_type=F32
    )
    weight_grad = lax.psum_scatter(
        terms * scale, ("node", "local"), scatter_dimension=0, tiled=True
    )
    return keys, token_grad, weight_grad, gain_grad


def solution(mesh):
    local_count = mesh.shape["local"]
    count = mesh.shape["node"] * local_count

    def local(tokens, norm_gain, key_weight, key_cotangent):
        scale = 1.0 / math.sqrt(tokens.shape[0] * count)
        if key_weight.shape[0] % 128 == 0 and count & (count - 1) == 0 and count >= 16:
            return fused(
                local_count, count, scale, tokens, norm_gain, key_weight, key_cotangent
            )
        return plain(scale, tokens, norm_gain, key_weight, key_cotangent)

    placed = P(("node", "local"), None)
    return jax.shard_map(
        local,
        mesh=mesh,
        in_specs=(placed, P(), placed, placed),
        out_specs=(placed, placed, placed, P()),
        check_vma=False,
    )
```

```python
import functools
import math

import jax
import jax.numpy as jnp
from jax import lax
from jax.experimental import pallas as pl
from jax.experimental.pallas import tpu as pltpu
from jax.sharding import PartitionSpec as P

MESH = pl.DeviceIdType.MESH
F32 = jnp.float32
BF16 = jnp.bfloat16


def stream_plan(bits):
    rest = list(range(1, bits))
    if bits == 5:
        return [3, 3, 2], [[0, 1, 2, 3, 4], [0, 2, 1, 3, 4], [0, 3, 4, 1, 2]]
    return [4, 4], [[0] + rest, [0] + rest[::-1]]


def gain_groups(bits):
    return [list(range(1, bits)), [0]]


def masks(group):
    return [
        sum(1 << k for n, k in enumerate(group) if m >> n & 1) for m in range(1, 1 << len(group))
    ]


def kernel(
    plan, local_count, scale, tok_hbm, gain_hbm, w_hbm, cot_hbm,
    keys_hbm, tg_hbm, wg_hbm, gg_hbm,
    keys_ref, tg_ref, wg_ref, gg_ref, tok, gain_ref, w_ref, cot_ref, hid, back, gains, rstds, rowco, gall, *rest,
):
    shares, orders = plan
    bits = len(orders[0])
    count = 1 << bits
    streams = len(shares)
    rows, heads = w_ref.shape
    toks, width = tok.shape
    wsize = [n * rows // 8 for n in shares]
    woff = [sum(wsize[:s]) for s in range(streams)]
    gsize = [n * heads // 8 for n in shares]
    goff = [sum(gsize[:s]) for s in range(streams)]
    it = iter(rest)
    wbuf = [next(it) for _ in range(streams)]
    acc = [next(it) for _ in range(streams)]
    send = [[None] + [next(it) for _ in range(1, bits)] for _ in range(streams)]
    recv = [[None] + [next(it) for _ in range(1, bits)] for _ in range(streams)]
    (sent, came) = next(it), next(it)
    (
        tok_sem, in_sem, out_sem, ag_send, ag_recv, fw_send, fw_recv,
        pair_send, pair_recv, rs_send, rs_recv, g_send, g_recv,
    ) = list(it)

    me = lax.axis_index("node") * local_count + lax.axis_index("local")
    flips = [(1 << k) * (1 - 2 * ((me // (1 << k)) % 2)) for k in range(bits)]

    def device(index):
        return (index // local_count, index % local_count)

    def partner(r):
        return device(block_of(r))

    def block_of(r):
        total = me
        for k in range(bits):
            if r >> k & 1:
                total = total + flips[k]
        return total

    def place(s, r):
        return sum((r >> k & 1) << (bits - 1 - j) for j, k in enumerate(orders[s]))

    def at_place(s, p):
        return sum(((p >> (bits - 1 - j)) & 1) << k for j, k in enumerate(orders[s]))

    def columns(i):
        return pl.ds(pl.multiple_of(i * rows, rows), rows)

    parts = rows // 128

    def gain_of(i):
        return jnp.concatenate(
            [gains[pl.ds(i * parts + j, 1), :] for j in range(parts)], axis=1
        )

    def across(ref):
        return jnp.concatenate([ref[...]] * parts, axis=1)

    w_copy = pltpu.make_async_copy(w_hbm, w_ref, in_sem.at[0])
    cot_copy = pltpu.make_async_copy(cot_hbm, cot_ref, in_sem.at[1])
    gain_copy_in = pltpu.make_async_copy(gain_hbm, gain_ref, in_sem.at[2])
    chunks = tok_sem.shape[0]
    cw = width // chunks
    tok_copies = [
        pltpu.make_async_copy(
            tok_hbm.at[:, pl.ds(c * cw, cw)], tok.at[:, pl.ds(c * cw, cw)], tok_sem.at[c]
        )
        for c in range(chunks)
    ]
    for copy in [w_copy] + tok_copies + [cot_copy, gain_copy_in]:
        copy.start()

    barrier = pltpu.get_barrier_semaphore()

    groups = gain_groups(bits)
    friends = sorted({r for g in groups for r in masks(g)})
    for r in friends:
        pl.semaphore_signal(barrier, inc=1, device_id=partner(r), device_id_type=MESH)
    w_copy.wait()
    for s in range(streams):
        wbuf[s][0] = w_ref[pl.ds(woff[s], wsize[s]), :]
    pl.semaphore_wait(barrier, len(friends))

    half, quarter = count // 2, count // 4

    def ag_copy(s, k):
        size = 1 << k
        return pltpu.make_async_remote_copy(
            src_ref=wbuf[s].at[pl.ds(0, size)],
            dst_ref=wbuf[s].at[pl.ds(size, size)],
            send_sem=ag_send.at[s, k],
            recv_sem=ag_recv.at[s, k],
            device_id=partner(1 << orders[s][bits - 1 - k]),
            device_id_type=MESH,
        )

    def forward(s, k):
        start, size = (1 << k) // 2, max(1, (1 << k) // 2)
        return pltpu.make_async_remote_copy(
            src_ref=wbuf[s].at[pl.ds(start, size)],
            dst_ref=wbuf[s].at[pl.ds(half + start, size)],
            send_sem=fw_send.at[s, k],
            recv_sem=fw_recv.at[s, k],
            device_id=partner(1),
            device_id_type=MESH,
        )

    def ag_step(k):
        for s in range(streams):
            if k:
                ag_copy(s, k - 1).wait_recv()
            if k < bits - 1:
                ag_copy(s, k).start()
            forward(s, k).start()

    def pair_copy(q):
        return pltpu.make_async_remote_copy(
            src_ref=sent.at[q],
            dst_ref=came.at[q],
            send_sem=pair_send.at[q],
            recv_sem=pair_recv.at[q],
            device_id=partner(1),
            device_id_type=MESH,
        )

    def rs_copy(s, k, c):
        size = count >> (k + 1)
        low = size // 2
        span = pl.ds(0, 1) if size == 1 else pl.ds(low * c, low)
        return pltpu.make_async_remote_copy(
            src_ref=send[s][k].at[span],
            dst_ref=recv[s][k].at[span],
            send_sem=rs_send.at[s, k, c],
            recv_sem=rs_recv.at[s, k, c],
            device_id=partner(1 << orders[s][k]),
            device_id_type=MESH,
        )

    def halves(k):
        return (1, 0) if count >> (k + 1) > 1 else (0,)

    def incoming(s, k, p):
        if k:
            return recv[s][k][p].astype(F32)
        return came[at_place(s, p) // 2, goff[s]: goff[s] + gsize[s], :].astype(F32)

    def rs_step(k):
        low = count >> (k + 2)
        if k == 0:
            for q in range(half):
                pair_copy(q).wait_recv()
        for s in range(streams):
            if k:
                rs_copy(s, k, 1).wait_recv()
            for c in halves(k + 1):
                size = max(1, low // 2)
                for p in range(c * size, (c + 1) * size):
                    send[s][k + 1][p] = (
                        acc[s][low + p] + incoming(s, k, low + p)
                    ).astype(BF16)
                rs_copy(s, k + 1, c).start()
        for s in range(streams):
            if k:
                rs_copy(s, k, 0).wait_recv()
            for p in range(low):
                acc[s][p] = acc[s][p] + incoming(s, k, p)

    ag_step(0)

    squares = jnp.zeros((toks, 128), F32)
    for c in range(chunks):
        tok_copies[c].wait()

        def square(j, total, c=c):
            part = tok[:, pl.ds(pl.multiple_of(c * cw + j * 512, 512), 512)].astype(F32)
            part = part * part
            return total + (
                (part[:, :128] + part[:, 128:256]) + (part[:, 256:384] + part[:, 384:])
            )

        squares = lax.fori_loop(0, cw // 512, square, squares)
    rstd = lax.rsqrt(jnp.sum(squares, axis=1, keepdims=True) * (1.0 / width) + 1e-05)
    rstds[...] = jnp.broadcast_to(rstd, rstds.shape)
    gain_copy_in.wait()
    gains[...] = gain_ref[...].astype(F32)
    cot_copy.wait()

    ag_step(1)

    cot_t = cot_ref[...].T

    def weight_terms(flip, begin, end):
        for q in range(begin, end):
            r = 2 * q + flip
            i = block_of(r)
            normed = tok[:, columns(i)].astype(F32) * across(rstds)
            hidden = (normed * gain_of(i)).astype(BF16)
            hid[:, columns(i)] = hidden
            terms = jnp.dot(cot_t, hidden, preferred_element_type=F32)
            if flip:
                sent[q] = terms.astype(BF16)
                pair_copy(q).start()
            else:
                for s in range(streams):
                    acc[s][place(s, r)] = terms[goff[s]: goff[s] + gsize[s]]

    weight_terms(1, 0, quarter)
    ag_step(2)
    weight_terms(1, quarter, half)
    weight_terms(0, 0, quarter)
    for k in range(3, bits - 1):
        ag_step(k)
    weight_terms(0, quarter, half)
    rs_step(0)

    def weight_pass(flip, begin, end, total):
        for q in range(begin, end):
            r = 2 * q + flip
            i = block_of(r)
            block = jnp.concatenate([wbuf[s][place(s, r)] for s in range(streams)], axis=0)
            dhidden = lax.dot_general(
                cot_ref[...], block, (((1,), (1,)), ((), ())), preferred_element_type=F32
            )
            back[:, columns(i)] = dhidden * gain_of(i) * across(rstds)
            total = total + jnp.dot(hid[:, columns(i)], block, preferred_element_type=F32)
        return total

    ag_step(bits - 1)
    total = weight_pass(0, 0, half, jnp.zeros((toks, heads), F32))
    rs_step(1)
    for s in range(streams):
        for k in range(bits):
            forward(s, k).wait_recv()
    total = weight_pass(1, 0, quarter, total)
    rs_step(2)
    total = weight_pass(1, quarter, half, total)
    for k in range(3, bits - 1):
        rs_step(k)

    keys_ref[...] = total.astype(BF16)
    outs = [pltpu.make_async_copy(keys_ref, keys_hbm, out_sem.at[1])]
    outs[-1].start()
    inner = jnp.sum(total * cot_ref[...].astype(F32), axis=1, keepdims=True) * (1.0 / width)
    rowco[...] = rstds[...] * rstds[...] * inner

    def token_part(i, carry):
        tg_ref[:, columns(i)] = (
            back[:, columns(i)] - tok[:, columns(i)].astype(F32) * across(rowco)
        ).astype(BF16)
        return carry

    def token_grad(g):
        lax.fori_loop(
            g * count // chunks, (g + 1) * count // chunks, token_part, 0, unroll=2
        )
        outs.append(
            pltpu.make_async_copy(
                tg_ref.at[:, pl.ds(g * cw, cw)], tg_hbm.at[:, pl.ds(g * cw, cw)],
                out_sem.at[3 + g],
            )
        )
        outs[-1].start()

    for g in range(chunks // 2):
        token_grad(g)

    sends, spans, ranks = [], [], [0]
    for g in groups:
        steps = masks(g)
        spans.append([(r, len(ranks) * (m + 1), len(ranks)) for m, r in enumerate(steps)])
        ranks = ranks + [x + r for r in steps for x in ranks]

    def gain_copies(phase):
        base = sum(len(span) for span in spans[:phase])
        return [
            pltpu.make_async_remote_copy(
                src_ref=gall.at[pl.ds(0, size)],
                dst_ref=gall.at[pl.ds(start, size)],
                send_sem=g_send.at[base + n],
                recv_sem=g_recv.at[base + n],
                device_id=partner(r),
                device_id_type=MESH,
            )
            for n, (r, start, size) in enumerate(spans[phase])
        ]

    def gain_step(phase):
        if phase:
            for copy in gain_copies(phase - 1):
                copy.wait_recv()
        if phase < len(groups):
            for copy in gain_copies(phase):
                copy.start()

    pieces = []
    for s in range(streams):
        rs_copy(s, bits - 1, 0).wait_recv()
        pieces.append((acc[s][0] + recv[s][bits - 1][0].astype(F32)) * scale)
    grad = jnp.concatenate(pieces, axis=0).T
    product = grad * w_ref[...].astype(F32)
    sums = lax.dot_general(
        jnp.ones((8, heads), F32), product, (((1,), (1,)), ((), ())),
        precision=lax.Precision.HIGHEST, preferred_element_type=F32,
    )
    own = sums[:1] / gain_of(me)
    gall[0] = own
    gain_step(0)

    wg_ref[...] = grad
    outs.append(pltpu.make_async_copy(wg_ref, wg_hbm, out_sem.at[0]))
    outs[-1].start()
    for g in range(chunks // 2, chunks):
        token_grad(g)
    gain_step(1)
    for phase in range(2, len(groups) + 1):
        gain_step(phase)
    for p, r in enumerate(ranks):
        i = block_of(r)
        for j in range(parts):
            gg_ref[pl.ds(i * parts + j, 1), :] = gall[p, :, j * 128: (j + 1) * 128]
    outs.append(pltpu.make_async_copy(gg_ref, gg_hbm, out_sem.at[2]))
    outs[-1].start()
    for s in range(streams):
        for k in range(bits):
            forward(s, k).wait_send()
            if k < bits - 1:
                ag_copy(s, k).wait_send()
            if k:
                for c in halves(k):
                    rs_copy(s, k, c).wait_send()
    for q in range(half):
        pair_copy(q).wait_send()
    for phase in range(len(groups)):
        for copy in gain_copies(phase):
            copy.wait_send()
    for copy in outs:
        copy.wait()


def hand_out(pieces, *refs):
    pairs = len(pieces)
    here, there, between, into, out = (
        refs[:pairs], refs[pairs: 2 * pairs], refs[2 * pairs: 3 * pairs], refs[-2], refs[-1]
    )
    cuts = []
    for n, parts in enumerate(pieces):
        rows = here[n].shape[0] // parts
        cuts += [(n, pl.ds(m * rows, rows)) for m in range(parts)]
    first = [
        pltpu.make_async_copy(here[n].at[cut], between[n].at[cut], into.at[c])
        for c, (n, cut) in enumerate(cuts)
    ]
    second = [
        pltpu.make_async_copy(between[n].at[cut], there[n].at[cut], out.at[c])
        for c, (n, cut) in enumerate(cuts)
    ]
    for copy in first:
        copy.start()
    for before, after in zip(first, second):
        before.wait()
        after.start()
    for copy in second:
        copy.wait()


def fused(local_count, count, scale, tokens, norm_gain, key_weight, key_cotangent):
    rows, heads = key_weight.shape
    toks, width = tokens.shape
    bits = count.bit_length() - 1
    plan = stream_plan(bits)
    shares, _ = plan
    hbm = pl.BlockSpec(memory_space=pltpu.HBM)
    anywhere = pl.BlockSpec(memory_space=pl.ANY)
    stages = [
        pltpu.VMEM((count >> (k + 1), n * heads // 8, rows), BF16)
        for n in shares
        for k in range(1, bits)
    ]
    pieces = [1, 8, 1, 1]
    shapes = (
        jax.ShapeDtypeStruct((toks, heads), BF16),
        jax.ShapeDtypeStruct((toks, width), BF16),
        jax.ShapeDtypeStruct((rows, heads), F32),
        jax.ShapeDtypeStruct((width // 128, 128), F32),
    )
    results = pl.pallas_call(
        functools.partial(kernel, plan, local_count, scale),
        out_shape=shapes,
        in_specs=[hbm] * 4,
        out_specs=[anywhere] * 4,
        scratch_shapes=[pltpu.VMEM(shape.shape, shape.dtype) for shape in shapes]
        + [
            pltpu.VMEM((toks, width), BF16),
            pltpu.VMEM((width // 128, 128), BF16),
            pltpu.VMEM((rows, heads), BF16),
            pltpu.VMEM((toks, heads), BF16),
            pltpu.VMEM((toks, width), BF16),
            pltpu.VMEM((toks, width), F32),
            pltpu.VMEM((width // 128, 128), F32),
            pltpu.VMEM((toks, 128), F32),
            pltpu.VMEM((toks, 128), F32),
            pltpu.VMEM((count, 1, rows), F32),
        ]
        + [pltpu.VMEM((count, n * rows // 8, heads), BF16) for n in shares]
        + [pltpu.VMEM((count // 2, n * heads // 8, rows), F32) for n in shares]
        + stages
        + stages
        + [pltpu.VMEM((count // 2, heads, rows), BF16)] * 2
        + [
            pltpu.SemaphoreType.DMA((4,)),
            pltpu.SemaphoreType.DMA((3,)),
            pltpu.SemaphoreType.DMA((7,)),
            pltpu.SemaphoreType.DMA((len(shares), bits)),
            pltpu.SemaphoreType.DMA((len(shares), bits)),
            pltpu.SemaphoreType.DMA((len(shares), bits)),
            pltpu.SemaphoreType.DMA((len(shares), bits)),
            pltpu.SemaphoreType.DMA((count // 2,)),
            pltpu.SemaphoreType.DMA((count // 2,)),
            pltpu.SemaphoreType.DMA((len(shares), bits, 2)),
            pltpu.SemaphoreType.DMA((len(shares), bits, 2)),
            pltpu.SemaphoreType.DMA((count // 2,)),
            pltpu.SemaphoreType.DMA((count // 2,)),
        ],
        compiler_params=pltpu.CompilerParams(
            collective_id=0, has_side_effects=True, vmem_limit_bytes=58 * 2**20
        ),
        cost_estimate=pl.CostEstimate(
            flops=6 * toks * width * heads, bytes_accessed=4 * toks * width, transcendentals=0
        ),
    )(tokens, norm_gain.reshape(width // 128, 128), key_weight, key_cotangent)
    keys, tg, wg, gg = pl.pallas_call(
        functools.partial(hand_out, pieces),
        out_shape=shapes,
        in_specs=[anywhere] * 4,
        out_specs=[hbm] * 4,
        scratch_shapes=[pltpu.VMEM(shape.shape, shape.dtype) for shape in shapes]
        + [pltpu.SemaphoreType.DMA((sum(pieces),))] * 2,
        compiler_params=pltpu.CompilerParams(vmem_limit_bytes=58 * 2**20),
        cost_estimate=pl.CostEstimate(
            flops=0, bytes_accessed=4 * toks * width, transcendentals=0
        ),
    )(*results)
    return keys, tg, wg, gg.reshape(width)


def plain(scale, tokens, norm_gain, key_weight, key_cotangent):
    gain_wide = norm_gain.astype(F32)
    wide = tokens.astype(F32)
    rstd = lax.rsqrt(jnp.mean(wide * wide, axis=1, keepdims=True) + 1e-05)
    normed = wide * rstd
    hidden = (normed * gain_wide).astype(BF16)
    whole = lax.all_gather(key_weight, ("node", "local"), axis=0, tiled=True)
    keys = jnp.dot(hidden, whole, preferred_element_type=F32).astype(BF16)
    dhidden = lax.dot_general(
        key_cotangent, whole, (((1,), (1,)), ((), ())), preferred_element_type=F32
    )
    dnormed = dhidden * gain_wide
    inner = jnp.mean(dnormed * normed, axis=1, keepdims=True)
    token_grad = (rstd * (dnormed - normed * inner)).astype(BF16)
    gain_grad = lax.psum(jnp.sum(dhidden * normed, axis=0) * scale, ("node", "local"))
    terms = lax.dot_general(
        hidden, key_cotangent, (((0,), (0,)), ((), ())), preferred_element_type=F32
    )
    weight_grad = lax.psum_scatter(
        terms * scale, ("node", "local"), scatter_dimension=0, tiled=True
    )
    return keys, token_grad, weight_grad, gain_grad


def solution(mesh):
    local_count = mesh.shape["local"]
    count = mesh.shape["node"] * local_count

    def local(tokens, norm_gain, key_weight, key_cotangent):
        scale = 1.0 / math.sqrt(tokens.shape[0] * count)
        if key_weight.shape[0] % 128 == 0 and count & (count - 1) == 0 and count >= 16:
            return fused(
                local_count, count, scale, tokens, norm_gain, key_weight, key_cotangent
            )
        return plain(scale, tokens, norm_gain, key_weight, key_cotangent)

    placed = P(("node", "local"), None)
    return jax.shard_map(
        local,
        mesh=mesh,
        in_specs=(placed, P(), placed, placed),
        out_specs=(placed, placed, placed, P()),
        check_vma=False,
    )
```

```python
import functools
import math

import jax
import jax.numpy as jnp
from jax import lax
from jax.experimental import pallas as pl
from jax.experimental.pallas import tpu as pltpu
from jax.sharding import PartitionSpec as P

MESH = pl.DeviceIdType.MESH
F32 = jnp.float32
BF16 = jnp.bfloat16


def stream_plan(bits):
    rest = list(range(1, bits))
    if bits == 5:
        return [3, 3, 2], [[0, 1, 2, 3, 4], [0, 2, 1, 3, 4], [0, 3, 4, 1, 2]]
    return [4, 4], [[0] + rest, [0] + rest[::-1]]


def gain_groups(bits):
    return [list(range(1, bits)), [0]]


def masks(group):
    return [
        sum(1 << k for n, k in enumerate(group) if m >> n & 1) for m in range(1, 1 << len(group))
    ]


def kernel(
    plan, local_count, scale, tok_hbm, gain_hbm, w_hbm, cot_hbm,
    keys_hbm, tg_hbm, wg_hbm, gg_hbm,
    keys_ref, tg_ref, wg_ref, gg_ref, tok, gain_ref, w_ref, cot_ref, hid, back, gains, rstds, rowco, gall, *rest,
):
    shares, orders = plan
    bits = len(orders[0])
    count = 1 << bits
    streams = len(shares)
    rows, heads = w_ref.shape
    toks, width = tok.shape
    wsize = [n * rows // 8 for n in shares]
    woff = [sum(wsize[:s]) for s in range(streams)]
    gsize = [n * heads // 8 for n in shares]
    goff = [sum(gsize[:s]) for s in range(streams)]
    it = iter(rest)
    wbuf = [next(it) for _ in range(streams)]
    acc = [next(it) for _ in range(streams)]
    send = [[None] + [next(it) for _ in range(1, bits)] for _ in range(streams)]
    recv = [[None] + [next(it) for _ in range(1, bits)] for _ in range(streams)]
    (sent, came) = next(it), next(it)
    (
        tok_sem, in_sem, out_sem, ag_send, ag_recv, fw_send, fw_recv,
        pair_send, pair_recv, rs_send, rs_recv, g_send, g_recv,
    ) = list(it)

    me = lax.axis_index("node") * local_count + lax.axis_index("local")
    flips = [(1 << k) * (1 - 2 * ((me // (1 << k)) % 2)) for k in range(bits)]

    def device(index):
        return (index // local_count, index % local_count)

    def partner(r):
        return device(block_of(r))

    def block_of(r):
        total = me
        for k in range(bits):
            if r >> k & 1:
                total = total + flips[k]
        return total

    def place(s, r):
        return sum((r >> k & 1) << (bits - 1 - j) for j, k in enumerate(orders[s]))

    def at_place(s, p):
        return sum(((p >> (bits - 1 - j)) & 1) << k for j, k in enumerate(orders[s]))

    def columns(i):
        return pl.ds(pl.multiple_of(i * rows, rows), rows)

    parts = rows // 128

    def gain_of(i):
        return jnp.concatenate(
            [gains[pl.ds(i * parts + j, 1), :] for j in range(parts)], axis=1
        )

    def across(ref):
        return jnp.concatenate([ref[...]] * parts, axis=1)

    w_copy = pltpu.make_async_copy(w_hbm, w_ref, in_sem.at[0])
    cot_copy = pltpu.make_async_copy(cot_hbm, cot_ref, in_sem.at[1])
    gain_copy_in = pltpu.make_async_copy(gain_hbm, gain_ref, in_sem.at[2])
    chunks = tok_sem.shape[0]
    cw = width // chunks
    tok_copies = [
        pltpu.make_async_copy(
            tok_hbm.at[:, pl.ds(c * cw, cw)], tok.at[:, pl.ds(c * cw, cw)], tok_sem.at[c]
        )
        for c in range(chunks)
    ]
    for copy in [w_copy] + tok_copies + [cot_copy, gain_copy_in]:
        copy.start()

    barrier = pltpu.get_barrier_semaphore()

    groups = gain_groups(bits)
    friends = sorted({r for g in groups for r in masks(g)})
    for r in friends:
        pl.semaphore_signal(barrier, inc=1, device_id=partner(r), device_id_type=MESH)
    w_copy.wait()
    for s in range(streams):
        wbuf[s][0] = w_ref[pl.ds(woff[s], wsize[s]), :]
    pl.semaphore_wait(barrier, len(friends))

    half, quarter = count // 2, count // 4

    def ag_copy(s, k):
        size = 1 << k
        return pltpu.make_async_remote_copy(
            src_ref=wbuf[s].at[pl.ds(0, size)],
            dst_ref=wbuf[s].at[pl.ds(size, size)],
            send_sem=ag_send.at[s, k],
            recv_sem=ag_recv.at[s, k],
            device_id=partner(1 << orders[s][bits - 1 - k]),
            device_id_type=MESH,
        )

    def forward(s, k):
        start, size = (1 << k) // 2, max(1, (1 << k) // 2)
        return pltpu.make_async_remote_copy(
            src_ref=wbuf[s].at[pl.ds(start, size)],
            dst_ref=wbuf[s].at[pl.ds(half + start, size)],
            send_sem=fw_send.at[s, k],
            recv_sem=fw_recv.at[s, k],
            device_id=partner(1),
            device_id_type=MESH,
        )

    def ag_step(k):
        for s in range(streams):
            if k:
                ag_copy(s, k - 1).wait_recv()
            if k < bits - 1:
                ag_copy(s, k).start()
            forward(s, k).start()

    def pair_copy(q):
        return pltpu.make_async_remote_copy(
            src_ref=sent.at[q],
            dst_ref=came.at[q],
            send_sem=pair_send.at[q],
            recv_sem=pair_recv.at[q],
            device_id=partner(1),
            device_id_type=MESH,
        )

    def rs_copy(s, k, c):
        size = count >> (k + 1)
        low = size // 2
        span = pl.ds(0, 1) if size == 1 else pl.ds(low * c, low)
        return pltpu.make_async_remote_copy(
            src_ref=send[s][k].at[span],
            dst_ref=recv[s][k].at[span],
            send_sem=rs_send.at[s, k, c],
            recv_sem=rs_recv.at[s, k, c],
            device_id=partner(1 << orders[s][k]),
            device_id_type=MESH,
        )

    def halves(k):
        return (1, 0) if count >> (k + 1) > 1 else (0,)

    def incoming(s, k, p):
        if k:
            return recv[s][k][p].astype(F32)
        return came[at_place(s, p) // 2, goff[s]: goff[s] + gsize[s], :].astype(F32)

    def rs_step(k):
        low = count >> (k + 2)
        if k == 0:
            for q in range(half):
                pair_copy(q).wait_recv()
        for s in range(streams):
            if k:
                rs_copy(s, k, 1).wait_recv()
            for c in halves(k + 1):
                size = max(1, low // 2)
                for p in range(c * size, (c + 1) * size):
                    send[s][k + 1][p] = (
                        acc[s][low + p] + incoming(s, k, low + p)
                    ).astype(BF16)
                rs_copy(s, k + 1, c).start()
        for s in range(streams):
            if k:
                rs_copy(s, k, 0).wait_recv()
            for p in range(low):
                acc[s][p] = acc[s][p] + incoming(s, k, p)

    ag_step(0)

    squares = jnp.zeros((toks, 128), F32)
    for c in range(chunks):
        if c == chunks // 2:
            ag_step(1)
        tok_copies[c].wait()

        def square(j, total, c=c):
            part = tok[:, pl.ds(pl.multiple_of(c * cw + j * 512, 512), 512)].astype(F32)
            part = part * part
            return total + (
                (part[:, :128] + part[:, 128:256]) + (part[:, 256:384] + part[:, 384:])
            )

        squares = lax.fori_loop(0, cw // 512, square, squares)
    rstd = lax.rsqrt(jnp.sum(squares, axis=1, keepdims=True) * (1.0 / width) + 1e-05)
    rstds[...] = jnp.broadcast_to(rstd, rstds.shape)
    gain_copy_in.wait()
    gains[...] = gain_ref[...].astype(F32)
    cot_copy.wait()

    cot_t = cot_ref[...].T

    def weight_terms(flip, begin, end):
        for q in range(begin, end):
            r = 2 * q + flip
            i = block_of(r)
            normed = tok[:, columns(i)].astype(F32) * across(rstds)
            hidden = (normed * gain_of(i)).astype(BF16)
            hid[:, columns(i)] = hidden
            terms = jnp.dot(cot_t, hidden, preferred_element_type=F32)
            if flip:
                sent[q] = terms.astype(BF16)
                pair_copy(q).start()
            else:
                for s in range(streams):
                    acc[s][place(s, r)] = terms[goff[s]: goff[s] + gsize[s]]

    weight_terms(1, 0, quarter)
    ag_step(2)
    weight_terms(1, quarter, half)
    weight_terms(0, 0, quarter)
    for k in range(3, bits - 1):
        ag_step(k)
    weight_terms(0, quarter, half)
    rs_step(0)

    def weight_pass(flip, begin, end, total):
        for q in range(begin, end):
            r = 2 * q + flip
            i = block_of(r)
            block = jnp.concatenate([wbuf[s][place(s, r)] for s in range(streams)], axis=0)
            dhidden = lax.dot_general(
                cot_ref[...], block, (((1,), (1,)), ((), ())), preferred_element_type=F32
            )
            back[:, columns(i)] = dhidden * gain_of(i) * across(rstds)
            total = total + jnp.dot(hid[:, columns(i)], block, preferred_element_type=F32)
        return total

    ag_step(bits - 1)
    total = weight_pass(0, 0, half, jnp.zeros((toks, heads), F32))
    rs_step(1)
    for s in range(streams):
        for k in range(bits):
            forward(s, k).wait_recv()
    total = weight_pass(1, 0, quarter, total)
    rs_step(2)
    total = weight_pass(1, quarter, half, total)
    for k in range(3, bits - 1):
        rs_step(k)

    keys_ref[...] = total.astype(BF16)
    outs = [pltpu.make_async_copy(keys_ref, keys_hbm, out_sem.at[1])]
    outs[-1].start()
    inner = jnp.sum(total * cot_ref[...].astype(F32), axis=1, keepdims=True) * (1.0 / width)
    rowco[...] = rstds[...] * rstds[...] * inner

    def token_part(i, carry):
        tg_ref[:, columns(i)] = (
            back[:, columns(i)] - tok[:, columns(i)].astype(F32) * across(rowco)
        ).astype(BF16)
        return carry

    def token_grad(g):
        lax.fori_loop(
            g * count // chunks, (g + 1) * count // chunks, token_part, 0, unroll=2
        )
        outs.append(
            pltpu.make_async_copy(
                tg_ref.at[:, pl.ds(g * cw, cw)], tg_hbm.at[:, pl.ds(g * cw, cw)],
                out_sem.at[3 + g],
            )
        )
        outs[-1].start()

    for g in range(chunks // 2):
        token_grad(g)

    sends, spans, ranks = [], [], [0]
    for g in groups:
        steps = masks(g)
        spans.append([(r, len(ranks) * (m + 1), len(ranks)) for m, r in enumerate(steps)])
        ranks = ranks + [x + r for r in steps for x in ranks]

    def gain_copies(phase):
        base = sum(len(span) for span in spans[:phase])
        return [
            pltpu.make_async_remote_copy(
                src_ref=gall.at[pl.ds(0, size)],
                dst_ref=gall.at[pl.ds(start, size)],
                send_sem=g_send.at[base + n],
                recv_sem=g_recv.at[base + n],
                device_id=partner(r),
                device_id_type=MESH,
            )
            for n, (r, start, size) in enumerate(spans[phase])
        ]

    def gain_step(phase):
        if phase:
            for copy in gain_copies(phase - 1):
                copy.wait_recv()
        if phase < len(groups):
            for copy in gain_copies(phase):
                copy.start()

    pieces = []
    for s in range(streams):
        rs_copy(s, bits - 1, 0).wait_recv()
        pieces.append((acc[s][0] + recv[s][bits - 1][0].astype(F32)) * scale)
    grad = jnp.concatenate(pieces, axis=0).T
    product = grad * w_ref[...].astype(F32)
    sums = lax.dot_general(
        jnp.ones((8, heads), F32), product, (((1,), (1,)), ((), ())),
        precision=lax.Precision.HIGHEST, preferred_element_type=F32,
    )
    own = sums[:1] / gain_of(me)
    gall[0] = own
    gain_step(0)

    wg_ref[...] = grad
    outs.append(pltpu.make_async_copy(wg_ref, wg_hbm, out_sem.at[0]))
    outs[-1].start()
    for g in range(chunks // 2, chunks):
        token_grad(g)
    gain_step(1)
    for phase in range(2, len(groups) + 1):
        gain_step(phase)
    for p, r in enumerate(ranks):
        i = block_of(r)
        for j in range(parts):
            gg_ref[pl.ds(i * parts + j, 1), :] = gall[p, :, j * 128: (j + 1) * 128]
    outs.append(pltpu.make_async_copy(gg_ref, gg_hbm, out_sem.at[2]))
    outs[-1].start()
    for s in range(streams):
        for k in range(bits):
            forward(s, k).wait_send()
            if k < bits - 1:
                ag_copy(s, k).wait_send()
            if k:
                for c in halves(k):
                    rs_copy(s, k, c).wait_send()
    for q in range(half):
        pair_copy(q).wait_send()
    for phase in range(len(groups)):
        for copy in gain_copies(phase):
            copy.wait_send()
    for copy in outs:
        copy.wait()


def hand_out(pieces, *refs):
    pairs = len(pieces)
    here, there, between, into, out = (
        refs[:pairs], refs[pairs: 2 * pairs], refs[2 * pairs: 3 * pairs], refs[-2], refs[-1]
    )
    cuts = []
    for n, parts in enumerate(pieces):
        rows = here[n].shape[0] // parts
        cuts += [(n, pl.ds(m * rows, rows)) for m in range(parts)]
    first = [
        pltpu.make_async_copy(here[n].at[cut], between[n].at[cut], into.at[c])
        for c, (n, cut) in enumerate(cuts)
    ]
    second = [
        pltpu.make_async_copy(between[n].at[cut], there[n].at[cut], out.at[c])
        for c, (n, cut) in enumerate(cuts)
    ]
    for copy in first:
        copy.start()
    for before, after in zip(first, second):
        before.wait()
        after.start()
    for copy in second:
        copy.wait()


def fused(local_count, count, scale, tokens, norm_gain, key_weight, key_cotangent):
    rows, heads = key_weight.shape
    toks, width = tokens.shape
    bits = count.bit_length() - 1
    plan = stream_plan(bits)
    shares, _ = plan
    hbm = pl.BlockSpec(memory_space=pltpu.HBM)
    anywhere = pl.BlockSpec(memory_space=pl.ANY)
    stages = [
        pltpu.VMEM((count >> (k + 1), n * heads // 8, rows), BF16)
        for n in shares
        for k in range(1, bits)
    ]
    pieces = [1, 8, 1, 1]
    shapes = (
        jax.ShapeDtypeStruct((toks, heads), BF16),
        jax.ShapeDtypeStruct((toks, width), BF16),
        jax.ShapeDtypeStruct((rows, heads), F32),
        jax.ShapeDtypeStruct((width // 128, 128), F32),
    )
    results = pl.pallas_call(
        functools.partial(kernel, plan, local_count, scale),
        out_shape=shapes,
        in_specs=[hbm] * 4,
        out_specs=[anywhere] * 4,
        scratch_shapes=[pltpu.VMEM(shape.shape, shape.dtype) for shape in shapes]
        + [
            pltpu.VMEM((toks, width), BF16),
            pltpu.VMEM((width // 128, 128), BF16),
            pltpu.VMEM((rows, heads), BF16),
            pltpu.VMEM((toks, heads), BF16),
            pltpu.VMEM((toks, width), BF16),
            pltpu.VMEM((toks, width), F32),
            pltpu.VMEM((width // 128, 128), F32),
            pltpu.VMEM((toks, 128), F32),
            pltpu.VMEM((toks, 128), F32),
            pltpu.VMEM((count, 1, rows), F32),
        ]
        + [pltpu.VMEM((count, n * rows // 8, heads), BF16) for n in shares]
        + [pltpu.VMEM((count // 2, n * heads // 8, rows), F32) for n in shares]
        + stages
        + stages
        + [pltpu.VMEM((count // 2, heads, rows), BF16)] * 2
        + [
            pltpu.SemaphoreType.DMA((4,)),
            pltpu.SemaphoreType.DMA((3,)),
            pltpu.SemaphoreType.DMA((7,)),
            pltpu.SemaphoreType.DMA((len(shares), bits)),
            pltpu.SemaphoreType.DMA((len(shares), bits)),
            pltpu.SemaphoreType.DMA((len(shares), bits)),
            pltpu.SemaphoreType.DMA((len(shares), bits)),
            pltpu.SemaphoreType.DMA((count // 2,)),
            pltpu.SemaphoreType.DMA((count // 2,)),
            pltpu.SemaphoreType.DMA((len(shares), bits, 2)),
            pltpu.SemaphoreType.DMA((len(shares), bits, 2)),
            pltpu.SemaphoreType.DMA((count // 2,)),
            pltpu.SemaphoreType.DMA((count // 2,)),
        ],
        compiler_params=pltpu.CompilerParams(
            collective_id=0, has_side_effects=True, vmem_limit_bytes=58 * 2**20
        ),
        cost_estimate=pl.CostEstimate(
            flops=6 * toks * width * heads, bytes_accessed=4 * toks * width, transcendentals=0
        ),
    )(tokens, norm_gain.reshape(width // 128, 128), key_weight, key_cotangent)
    keys, tg, wg, gg = pl.pallas_call(
        functools.partial(hand_out, pieces),
        out_shape=shapes,
        in_specs=[anywhere] * 4,
        out_specs=[hbm] * 4,
        scratch_shapes=[pltpu.VMEM(shape.shape, shape.dtype) for shape in shapes]
        + [pltpu.SemaphoreType.DMA((sum(pieces),))] * 2,
        compiler_params=pltpu.CompilerParams(vmem_limit_bytes=58 * 2**20),
        cost_estimate=pl.CostEstimate(
            flops=0, bytes_accessed=4 * toks * width, transcendentals=0
        ),
    )(*results)
    return keys, tg, wg, gg.reshape(width)


def plain(scale, tokens, norm_gain, key_weight, key_cotangent):
    gain_wide = norm_gain.astype(F32)
    wide = tokens.astype(F32)
    rstd = lax.rsqrt(jnp.mean(wide * wide, axis=1, keepdims=True) + 1e-05)
    normed = wide * rstd
    hidden = (normed * gain_wide).astype(BF16)
    whole = lax.all_gather(key_weight, ("node", "local"), axis=0, tiled=True)
    keys = jnp.dot(hidden, whole, preferred_element_type=F32).astype(BF16)
    dhidden = lax.dot_general(
        key_cotangent, whole, (((1,), (1,)), ((), ())), preferred_element_type=F32
    )
    dnormed = dhidden * gain_wide
    inner = jnp.mean(dnormed * normed, axis=1, keepdims=True)
    token_grad = (rstd * (dnormed - normed * inner)).astype(BF16)
    gain_grad = lax.psum(jnp.sum(dhidden * normed, axis=0) * scale, ("node", "local"))
    terms = lax.dot_general(
        hidden, key_cotangent, (((0,), (0,)), ((), ())), preferred_element_type=F32
    )
    weight_grad = lax.psum_scatter(
        terms * scale, ("node", "local"), scatter_dimension=0, tiled=True
    )
    return keys, token_grad, weight_grad, gain_grad


def solution(mesh):
    local_count = mesh.shape["local"]
    count = mesh.shape["node"] * local_count

    def local(tokens, norm_gain, key_weight, key_cotangent):
        scale = 1.0 / math.sqrt(tokens.shape[0] * count)
        if key_weight.shape[0] % 128 == 0 and count & (count - 1) == 0 and count >= 16:
            return fused(
                local_count, count, scale, tokens, norm_gain, key_weight, key_cotangent
            )
        return plain(scale, tokens, norm_gain, key_weight, key_cotangent)

    placed = P(("node", "local"), None)
    return jax.shard_map(
        local,
        mesh=mesh,
        in_specs=(placed, P(), placed, placed),
        out_specs=(placed, placed, placed, P()),
        check_vma=False,
    )
```
